32 devices in a mesh: space: 8 (over z, y), bin: 4 (over x, core).
Axes of the slice: x: 2, y: 2, z: 4, core: 2. Of those that a mesh axis runs over, the one named last changes fastest.
Arguments:
- spectrum: float32 [768, 320, 256], P('bin', 'space'), may hold values from 0.05 to 2
- sea_mask: int32 [320, 256], P('space'), may hold values 0 or 1
- wind_speed: float32 [320, 256], P('space'), may hold values from 5 to 25
- wind_heading: float32 [320, 256], P('space'), may hold values from -3.140625 to 3.140625
- quad: bfloat16 [768, 768], replicated, may hold values from -0.21875 to 0.21875
Outputs:
- new_spectrum: float32 [768, 320, 256], P('bin', 'space')
The draws below stay inside these ranges and needn't reach their ends.
All inputs are finite; a program needn't handle non-finite values. No bound on the sum of `sea_mask` on one device may be relied on, other than what follows from the above.
Results may differ from the reference program's by a relative error of at most 0.0003.
The reference program's roundings to bfloat16 on the way count: a program that leaves them out, or rounds other values in their place, can miss the bound.
Values sent between devices are 32-bit elements; how exact they have to be, the bound alone decides.
A program may use at most 128 MiB of HBM per device.

```python
import math
import jax
import jax.numpy as jnp
from jax import lax

FREQS = 32
DIRS = 24
ROWS = 40
COLS = 256
BINS = 768
NX = 320
NY = 256
N_BIN = 4


def set_ends(array, rng, low, top_value):
    index_at = [jax.random.randint(jax.random.fold_in(rng, axis), (), 0, length) for axis, length in enumerate(array.shape)]
    main_axis = array.shape.index(max(array.shape))
    beside = index_at[:main_axis] + [(index_at[main_axis] + 1) % array.shape[main_axis]] + index_at[main_axis + 1:]
    return array.at[tuple(index_at)].set(low).at[tuple(beside)].set(top_value)


def level_of(key, extent, pieces, smallest, largest):
    def one(position, blocks):
        heights = jax.random.uniform(jax.random.fold_in(jax.random.fold_in(key, 6), position), (blocks,), jnp.float32, smallest / len(pieces), largest / len(pieces))
        return jnp.repeat(jnp.exp(heights), extent[position] // blocks).reshape((-1,) + (1,) * (len(extent) - position - 1))

    level = one(*pieces[0])
    for cut in pieces[1:]:
        level = level * one(*cut)
    return level


def normal_values(rng, shape, spread, bound, held_as=jnp.bfloat16):
    return jnp.clip(spread * jax.random.normal(rng, shape, jnp.float32), -bound, bound).astype(held_as)


def setup_inputs(seed: int = 0) -> dict:
    streams_of = jax.random.split(jax.random.key(seed), 6)
    return {
        "spectrum": jnp.clip(jnp.exp(math.log(2.0) - 3.6888794 * jax.random.uniform(streams_of[0], (BINS, NX, NY), jnp.float32) ** level_of(streams_of[0], (BINS, NX, NY), ((0, 4), (1, 8)), -0.2, 0.2)), 0.05, 2.0),
        "sea_mask": set_ends((jax.random.randint(streams_of[1], (NX, NY), 0, 8) < 7).astype(jnp.int32), jax.random.fold_in(streams_of[1], 1), 0, 1),
        "wind_speed": jnp.clip(jnp.exp(math.log(25.0) - 1.609438 * jax.random.uniform(streams_of[2], (NX, NY), jnp.float32) ** level_of(streams_of[2], (NX, NY), ((0, 8),), -0.2, 0.2)), 5.0, 25.0),
        "wind_heading": jnp.clip(jax.random.uniform(streams_of[3], (NX, NY), jnp.float32, -3.140625, 3.140625), -3.140625, 3.140625),
        "quad": normal_values(streams_of[4], (BINS, BINS), BINS ** -0.5, 0.21875),
    }


LOG_RATIO = math.log(1.1)
TWO_PI = 2.0 * math.pi
TIME_STEP = 0.2
NONLINEAR = 1.5
DAMPING = 2.0
GROWTH = 0.15


def bin_tables(bin_index):
    freq_level = (bin_index // DIRS).astype(jnp.float32)
    direction = (bin_index % DIRS).astype(jnp.float32)
    frequency = 0.04 * jnp.exp(freq_level * LOG_RATIO)
    courant = 0.65 * jnp.exp(-freq_level * LOG_RATIO)
    theta = (direction + 0.5) * (TWO_PI / DIRS)
    cos_theta = jnp.cos(theta)
    sin_theta = jnp.sin(theta)
    return frequency, courant * cos_theta, courant * sin_theta, cos_theta, sin_theta


def substep(padded, sea_rows, x_speed, y_speed):
    center = padded[:, 1:-1]
    back_row = padded[:, :-2]
    next_row = padded[:, 2:]
    sided = jnp.pad(center, ((0, 0), (0, 0), (1, 1)))
    left_col = sided[:, :, :-2]
    right_col = sided[:, :, 2:]
    updated = center - jnp.maximum(x_speed, 0.0) * (center - back_row)
    updated = updated - jnp.minimum(x_speed, 0.0) * (next_row - center)
    updated = updated - jnp.maximum(y_speed, 0.0) * (center - left_col)
    updated = updated - jnp.minimum(y_speed, 0.0) * (right_col - center)
    return updated * sea_rows


def reflect(values):
    count = values.shape[1]
    return values.reshape(FREQS, DIRS, count)[:, ::-1].reshape(FREQS * DIRS, count)


def sources(energy, quad, frequency):
    count = energy.shape[1]
    low = energy.astype(jnp.bfloat16)
    coupled = jnp.dot(quad, jnp.concatenate([low, reflect(low)], axis=1), preferred_element_type=jnp.float32)
    transfer = NONLINEAR * energy * (coupled[:, :count] + reflect(coupled[:, count:]))
    total = jnp.sum(energy, axis=0) / BINS
    top_freq = 0.04 * math.exp((FREQS - 1) * LOG_RATIO)
    steep = frequency / top_freq
    dissipation = -DAMPING * (steep * steep)[:, None] * energy * (total * total)[None, :]
    return transfer + dissipation


def wind_growth(energy, frequency, cos_theta, sin_theta, speed, heading):
    along = cos_theta * jnp.cos(heading) + sin_theta * jnp.sin(heading)
    rate = GROWTH * jnp.maximum(0.77 * speed * frequency * along - 1.0, 0.0)
    return rate * energy


def reference(spectrum, sea_mask, wind_speed, wind_heading, quad):
    frequency, x_table, y_table, cos_theta, sin_theta = bin_tables(jnp.arange(BINS, dtype=jnp.int32))
    sea_rows = sea_mask.astype(jnp.float32)

    def propagate(packed):
        current, x_speed, y_speed = packed
        for sweep in range(3):
            padded = jnp.pad(current, ((0, 0), (1, 1), (0, 0)))
            current = substep(padded, sea_rows, x_speed[:, None, None], y_speed[:, None, None])
        return current

    propagated = lax.map(propagate, (spectrum.reshape(FREQS, DIRS, NX, NY), x_table.reshape(FREQS, DIRS), y_table.reshape(FREQS, DIRS)))
    flat = propagated.reshape(BINS, NX * NY)
    speeds = wind_speed.reshape(1, NX * NY)
    headings = wind_heading.reshape(1, NX * NY)
    block_size = ROWS * COLS // N_BIN

    def update(block_id, field):
        start = (block_id * block_size).astype(jnp.int32)
        energy = lax.dynamic_slice_in_dim(field, start, block_size, 1)
        speed = lax.dynamic_slice_in_dim(speeds, start, block_size, 1)
        heading = lax.dynamic_slice_in_dim(headings, start, block_size, 1)
        growth = wind_growth(energy, frequency[:, None], cos_theta[:, None], sin_theta[:, None], speed, heading)
        updated = energy + TIME_STEP * (growth + sources(energy, quad, frequency))
        return lax.dynamic_update_slice_in_dim(field, updated, start, 1)

    result = lax.fori_loop(0, NX * NY // block_size, update, flat)
    return result.reshape(BINS, NX, NY)
```

```python
import functools
import math

import jax
import jax.numpy as jnp
import numpy as np
from jax import lax
from jax.experimental import pallas as pl
from jax.experimental.pallas import tpu as pltpu
from jax.sharding import PartitionSpec as P

FREQS = 32
DIRS = 24
BINS = 768

LOG_RATIO = math.log(1.1)
TWO_PI = 2.0 * math.pi
TIME_STEP = 0.2
NONLINEAR = 1.5
DAMPING = 2.0
GROWTH = 0.15

HALO = 3
TILE = 8
UNIT = 2

AX, AY, XPOS, YPOS, FCOS, FSIN, STEEP2 = range(7)


def bin_tables():
    bins = np.arange(BINS)
    level = (bins // DIRS).astype(np.float64)
    direction = (bins % DIRS).astype(np.float64)
    frequency = 0.04 * np.exp(level * LOG_RATIO)
    courant = 0.65 * np.exp(-level * LOG_RATIO)
    theta = (direction + 0.5) * (TWO_PI / DIRS)
    cos_theta, sin_theta = np.cos(theta), np.sin(theta)
    top_freq = 0.04 * math.exp((FREQS - 1) * LOG_RATIO)
    table = np.zeros((BINS, 128), np.float32)
    table[:, AX] = np.abs(courant * cos_theta)
    table[:, AY] = np.abs(courant * sin_theta)
    table[:, XPOS] = cos_theta > 0
    table[:, YPOS] = sin_theta > 0
    table[:, FCOS] = frequency * cos_theta
    table[:, FSIN] = frequency * sin_theta
    table[:, STEEP2] = (frequency / top_freq) ** 2
    return table


def reversal(rows, row_start, cols, col_start):
    i = lax.broadcasted_iota(jnp.int32, (rows, cols), 0).astype(jnp.float32) + row_start
    j = lax.broadcasted_iota(jnp.int32, (rows, cols), 1).astype(jnp.float32) + col_start
    level = jnp.floor((i + 0.5) * (1.0 / DIRS))
    return jnp.where(i + j == 2 * DIRS * level + (DIRS - 1), 1.0, 0.0).astype(jnp.bfloat16)


def kernel(
    n, s, spec, mask, speed, heading, quad, table, out,
    ext, mask_s, u_s, v_s, every, q2, tab,
    load_sem, halo_send, halo_recv, x_send, x_recv, f_send, f_recv, out_sem,
):
    rows, nb, cols = spec.shape
    tiles = rows // TILE
    units = rows // UNIT
    chips = n // 2
    b = lax.axis_index("bin")
    sp = lax.axis_index("space")
    chip, core = b // 2, lax.rem(b, 2)
    sibling = chip * 2 + 1 - core

    def far_to(k):
        return lax.rem(chip + k, chips) * 2 + core

    def far_from(k):
        return lax.rem(chip + chips - k, chips) * 2 + core

    loads = [
        pltpu.make_async_copy(
            spec.at[pl.ds(t * TILE, TILE)], ext.at[pl.ds(HALO + t * TILE, TILE)], load_sem.at[t]
        )
        for t in range(tiles)
    ]
    for load in loads:
        load.start()
    tab_load = pltpu.make_async_copy(
        table.at[pl.ds(pl.multiple_of(b * nb, 16), nb)], tab, load_sem.at[tiles]
    )
    tab_load.start()
    q_load = pltpu.make_async_copy(
        quad.at[pl.ds(pl.multiple_of(b * nb, 16), nb)], q2.at[pl.ds(0, nb)], load_sem.at[tiles + 1]
    )
    q_load.start()

    barrier = pltpu.get_barrier_semaphore()
    pl.semaphore_signal(barrier, 1, device_id={"bin": sibling})
    for k in range(1, chips):
        pl.semaphore_signal(barrier, 1, device_id={"bin": far_to(k)})

    @pl.when(sp > 0)
    def _():
        pl.semaphore_signal(barrier, 1, device_id={"space": sp - 1})

    @pl.when(sp < s - 1)
    def _():
        pl.semaphore_signal(barrier, 1, device_id={"space": sp + 1})

    mask_f = mask[...].astype(jnp.float32)
    u_all = 0.77 * speed[...] * jnp.cos(heading[...])
    v_all = 0.77 * speed[...] * jnp.sin(heading[...])
    for r in range(rows):
        mask_s[HALO + r] = mask_f[r : r + 1]
        u_s[r] = u_all[r : r + 1]
        v_s[r] = v_all[r : r + 1]

    pl.semaphore_wait(barrier, chips + jnp.minimum(sp, 1) + jnp.minimum(s - 1 - sp, 1))

    up = {"space": sp + 1}
    down = {"space": sp - 1}
    to_up = [
        pltpu.make_async_remote_copy(
            spec.at[pl.ds(rows - HALO, HALO)], ext.at[pl.ds(0, HALO)],
            halo_send.at[0], halo_recv.at[0], device_id=up,
        ),
        pltpu.make_async_remote_copy(
            mask_s.at[pl.ds(rows, HALO)], mask_s.at[pl.ds(0, HALO)],
            halo_send.at[1], halo_recv.at[1], device_id=up,
        ),
    ]
    to_down = [
        pltpu.make_async_remote_copy(
            spec.at[pl.ds(0, HALO)], ext.at[pl.ds(rows + HALO, HALO)],
            halo_send.at[2], halo_recv.at[2], device_id=down,
        ),
        pltpu.make_async_remote_copy(
            mask_s.at[pl.ds(HALO, HALO)], mask_s.at[pl.ds(rows + HALO, HALO)],
            halo_send.at[3], halo_recv.at[3], device_id=down,
        ),
    ]

    @pl.when(sp < s - 1)
    def _():
        for copy in to_up:
            copy.start()

    @pl.when(sp > 0)
    def _():
        for copy in to_down:
            copy.start()

    @pl.when(sp == 0)
    def _():
        ext[pl.ds(0, HALO)] = jnp.zeros((HALO, nb, cols), jnp.float32)
        mask_s[pl.ds(0, HALO)] = jnp.zeros((HALO, 1, cols), jnp.float32)

    @pl.when(sp == s - 1)
    def _():
        ext[pl.ds(rows + HALO, HALO)] = jnp.zeros((HALO, nb, cols), jnp.float32)
        mask_s[pl.ds(rows + HALO, HALO)] = jnp.zeros((HALO, 1, cols), jnp.float32)

    def start_row(j):
        done = j * UNIT
        return lax.rem(done // TILE + 1, tiles) * TILE + lax.rem(done, TILE)

    def block(j, owner):
        return every.at[
            pl.ds(start_row(j), UNIT), pl.ds(pl.multiple_of(owner * nb, 16), nb)
        ]

    def far_copy(j, k, owner):
        part = block(j, owner)
        return pltpu.make_async_remote_copy(
            part, part, x_send.at[j, k], x_recv.at[j, k], device_id={"bin": far_to(k)}
        )

    def near_copy(j, k, owner):
        part = block(j, owner)
        return pltpu.make_async_remote_copy(
            part, part, f_send.at[j, k], f_recv.at[j, k], device_id={"bin": sibling}
        )

    def other(owner):
        return owner + 1 - 2 * core

    tab_load.wait()
    lane = lax.broadcasted_iota(jnp.int32, (8, cols), 1)

    def propagate(t):
        base = t * TILE

        def group(g, carry):
            at = pl.multiple_of(g * 8, 8)
            coef = tab[pl.ds(at, 8)]

            def wide(col):
                return jnp.broadcast_to(coef[:, col : col + 1], (8, cols))

            ax, ay = wide(AX), wide(AY)
            xpos, ypos = wide(XPOS) > 0.5, wide(YPOS) > 0.5
            edge = jnp.where(
                jnp.where(ypos, lane, cols - 1 - lane) == 0, 0.0, 1.0
            )
            field = [ext[base + m, pl.ds(at, 8)] for m in range(TILE + 2 * HALO)]
            for step in range(3):
                new = []
                for m in range(1, len(field) - 1):
                    e = field[m]
                    back = jnp.where(xpos, field[m - 1], field[m + 1])
                    side = edge * jnp.where(
                        ypos, pltpu.roll(e, 1, 1), pltpu.roll(e, cols - 1, 1)
                    )
                    value = e - ax * (e - back) - ay * (e - side)
                    new.append(value * mask_s[base + m + step])
                field = new
            where = pl.multiple_of(b * nb + at, 8)
            for m in range(TILE):
                every[base + m, pl.ds(where, 8)] = field[m]
            return carry

        lax.fori_loop(0, nb // 8, group, 0)

    def tile_step(i, carry):
        t = lax.rem(i + 1, tiles)

        @pl.when(i == 0)
        def _():
            for load in loads[:3]:
                load.wait()

        for later in range(3, tiles):

            @pl.when(i == later - 2)
            def _():
                loads[later].wait()

        @pl.when(i == tiles - 2)
        def _():
            @pl.when(sp > 0)
            def _():
                for copy in to_up:
                    copy.wait_recv()

            @pl.when(sp < s - 1)
            def _():
                for copy in to_down:
                    copy.wait_recv()

        propagate(t)

        def send(p, carry):
            j = i * (TILE // UNIT) + p
            for k in range(1, chips):
                far_copy(j, k, b).start()
            near_copy(j, 0, b).start()
            return carry

        lax.fori_loop(0, TILE // UNIT, send, 0)
        return carry

    lax.fori_loop(0, tiles, tile_step, 0)

    q_load.wait()
    turned = jnp.dot(
        reversal(nb, 0, nb, 0), q2[pl.ds(0, nb)], preferred_element_type=jnp.float32
    ).astype(jnp.bfloat16)
    for c in range(BINS // 256):
        q2[pl.ds(nb, nb), pl.ds(c * 256, 256)] = jnp.dot(
            turned, reversal(BINS, 0, 256, c * 256), preferred_element_type=jnp.float32
        ).astype(jnp.bfloat16)

    own = pl.ds(pl.multiple_of(b * nb, 16), nb)

    def compute(row):
        total = jnp.sum(every[row], axis=0, keepdims=True) * (1.0 / BINS)
        low = every[row].astype(jnp.bfloat16)
        coupled = jnp.dot(q2[...], low, preferred_element_type=jnp.float32)
        energy = every[row, own]
        along = tab[:, FCOS : FCOS + 1] * u_s[row] + tab[:, FSIN : FSIN + 1] * v_s[row]
        growth = GROWTH * jnp.maximum(along - 1.0, 0.0)
        rate = (
            growth
            + NONLINEAR * (coupled[:nb] + coupled[nb:])
            - DAMPING * tab[:, STEEP2 : STEEP2 + 1] * (total * total)
        )
        ext[HALO + row] = energy + TIME_STEP * (rate * energy)

    def out_copy(j):
        row = start_row(j)
        return pltpu.make_async_copy(
            ext.at[pl.ds(HALO + row, UNIT)], out.at[pl.ds(row, UNIT)], out_sem.at[j]
        )

    def unit_step(j, carry):
        @pl.when(j < units)
        def _():
            for k in range(1, chips):
                far_copy(j, k, far_from(k)).wait_recv()
                near_copy(j, k, far_from(k)).start()

        @pl.when(j > 0)
        def _():
            near_copy(j - 1, 0, sibling).wait_recv()
            for k in range(1, chips):
                near_copy(j - 1, k, other(far_from(k))).wait_recv()
            for r in range(UNIT):
                compute(start_row(j - 1) + r)
            out_copy(j - 1).start()

        return carry

    lax.fori_loop(0, units + 1, unit_step, 0)

    def drain(j, carry):
        for k in range(1, chips):
            far_copy(j, k, b).wait_send()
            near_copy(j, k, far_from(k)).wait_send()
        near_copy(j, 0, b).wait_send()
        out_copy(j).wait()
        return carry

    lax.fori_loop(0, units, drain, 0)

    @pl.when(sp < s - 1)
    def _():
        for copy in to_up:
            copy.wait_send()

    @pl.when(sp > 0)
    def _():
        for copy in to_down:
            copy.wait_send()


def on_device(n, s, spectrum, sea_mask, wind_speed, wind_heading, quad):
    nb, rows, cols = spectrum.shape
    units, chips, tiles = rows // UNIT, n // 2, rows // TILE
    vmem = pl.BlockSpec(memory_space=pltpu.VMEM)
    hbm = pl.BlockSpec(memory_space=pl.ANY)
    result = pl.pallas_call(
        functools.partial(kernel, n, s),
        out_shape=jax.ShapeDtypeStruct((rows, nb, cols), jnp.float32),
        in_specs=[hbm, vmem, vmem, vmem, hbm, hbm],
        out_specs=hbm,
        scratch_shapes=[
            pltpu.VMEM((rows + 2 * HALO, nb, cols), jnp.float32),
            pltpu.VMEM((rows + 2 * HALO, 1, cols), jnp.float32),
            pltpu.VMEM((rows, 1, cols), jnp.float32),
            pltpu.VMEM((rows, 1, cols), jnp.float32),
            pltpu.VMEM((rows, BINS, cols), jnp.float32),
            pltpu.VMEM((2 * nb, BINS), jnp.bfloat16),
            pltpu.VMEM((nb, 128), jnp.float32),
            pltpu.SemaphoreType.DMA((tiles + 2,)),
            pltpu.SemaphoreType.DMA((4,)),
            pltpu.SemaphoreType.DMA((4,)),
            pltpu.SemaphoreType.DMA((units, chips)),
            pltpu.SemaphoreType.DMA((units, chips)),
            pltpu.SemaphoreType.DMA((units, chips)),
            pltpu.SemaphoreType.DMA((units, chips)),
            pltpu.SemaphoreType.DMA((units,)),
        ],
        compiler_params=pltpu.CompilerParams(
            collective_id=0, has_side_effects=True, vmem_limit_bytes=60 * 1024 * 1024
        ),
        cost_estimate=pl.CostEstimate(
            flops=4 * nb * BINS * rows * cols, bytes_accessed=8 * nb * rows * cols, transcendentals=0
        ),
        name="wave_step",
    )(
        jnp.transpose(spectrum, (1, 0, 2)), sea_mask, wind_speed, wind_heading, quad,
        jnp.asarray(bin_tables()),
    )
    return jnp.transpose(result, (1, 0, 2))


def solution(mesh):
    return jax.shard_map(
        functools.partial(on_device, mesh.shape["bin"], mesh.shape["space"]),
        mesh=mesh,
        in_specs=(
            P("bin", "space", None),
            P("space", None),
            P("space", None),
            P("space", None),
            P(),
        ),
        out_specs=P("bin", "space", None),
        check_vma=False,
    )
```

```python
import functools
import math

import jax
import jax.numpy as jnp
import numpy as np
from jax import lax
from jax.experimental import pallas as pl
from jax.experimental.pallas import tpu as pltpu
from jax.sharding import PartitionSpec as P

FREQS = 32
DIRS = 24
BINS = 768

LOG_RATIO = math.log(1.1)
TWO_PI = 2.0 * math.pi
TIME_STEP = 0.2
NONLINEAR = 1.5
DAMPING = 2.0
GROWTH = 0.15

HALO = 3
CHUNK = 8
TILE = 4
UNIT = 2

AX, AY, XPOS, YPOS, FCOS, FSIN, STEEP2 = range(7)


def bin_tables():
    bins = np.arange(BINS)
    level = (bins // DIRS).astype(np.float64)
    direction = (bins % DIRS).astype(np.float64)
    frequency = 0.04 * np.exp(level * LOG_RATIO)
    courant = 0.65 * np.exp(-level * LOG_RATIO)
    theta = (direction + 0.5) * (TWO_PI / DIRS)
    cos_theta, sin_theta = np.cos(theta), np.sin(theta)
    top_freq = 0.04 * math.exp((FREQS - 1) * LOG_RATIO)
    table = np.zeros((BINS, 128), np.float32)
    table[:, AX] = np.abs(courant * cos_theta)
    table[:, AY] = np.abs(courant * sin_theta)
    table[:, XPOS] = cos_theta > 0
    table[:, YPOS] = sin_theta > 0
    table[:, FCOS] = frequency * cos_theta
    table[:, FSIN] = frequency * sin_theta
    table[:, STEEP2] = (frequency / top_freq) ** 2
    return table


def reversal(rows, row_start, cols, col_start):
    i = lax.broadcasted_iota(jnp.int32, (rows, cols), 0).astype(jnp.float32) + row_start
    j = lax.broadcasted_iota(jnp.int32, (rows, cols), 1).astype(jnp.float32) + col_start
    level = jnp.floor((i + 0.5) * (1.0 / DIRS))
    return jnp.where(i + j == 2 * DIRS * level + (DIRS - 1), 1.0, 0.0).astype(jnp.bfloat16)


def kernel(
    n, s, spec, mask, speed, heading, quad, table, out,
    nat, ext, mask_s, u_s, v_s, every, q2, tab,
    load_sem, halo_send, halo_recv, x_send, x_recv, f_send, f_recv, out_sem,
):
    nb, rows, cols = spec.shape
    tiles = rows // TILE
    chunks = rows // CHUNK
    units = rows // UNIT
    chips = n // 2
    b = lax.axis_index("bin")
    sp = lax.axis_index("space")
    chip, core = b // 2, lax.rem(b, 2)
    sibling = chip * 2 + 1 - core

    def far_to(k):
        return lax.rem(chip + k, chips) * 2 + core

    def far_from(k):
        return lax.rem(chip + chips - k, chips) * 2 + core

    loads = [
        pltpu.make_async_copy(
            spec.at[:, pl.ds(c * CHUNK, CHUNK)], nat.at[c], load_sem.at[c]
        )
        for c in range(chunks)
    ]
    for load in loads:
        load.start()
    tab_load = pltpu.make_async_copy(
        table.at[pl.ds(pl.multiple_of(b * nb, 16), nb)], tab, load_sem.at[chunks]
    )
    tab_load.start()
    q_load = pltpu.make_async_copy(
        quad.at[pl.ds(pl.multiple_of(b * nb, 16), nb)], q2.at[pl.ds(0, nb)], load_sem.at[chunks + 1]
    )
    q_load.start()

    barrier = pltpu.get_barrier_semaphore()
    pl.semaphore_signal(barrier, 1, device_id={"bin": sibling})
    for k in range(1, chips):
        pl.semaphore_signal(barrier, 1, device_id={"bin": far_to(k)})

    @pl.when(sp > 0)
    def _():
        pl.semaphore_signal(barrier, 1, device_id={"space": sp - 1})

    @pl.when(sp < s - 1)
    def _():
        pl.semaphore_signal(barrier, 1, device_id={"space": sp + 1})

    mask_f = mask[...].astype(jnp.float32)
    for r in range(rows):
        mask_s[HALO + r] = mask_f[r : r + 1]

    def to_rows(c):
        def group(g, carry):
            at = pl.ds(pl.multiple_of(g * 8, 8), 8)
            ext[pl.ds(HALO + c * CHUNK, CHUNK), at] = jnp.swapaxes(nat[c, at], 0, 1)
            return carry

        lax.fori_loop(0, nb // 8, group, 0)

    def to_bins(c):
        def group(g, carry):
            at = pl.ds(pl.multiple_of(g * 8, 8), 8)
            nat[c, at] = jnp.swapaxes(ext[pl.ds(HALO + c * CHUNK, CHUNK), at], 0, 1)
            return carry

        lax.fori_loop(0, nb // 8, group, 0)

    for c in range(2):
        loads[c].wait()
        to_rows(c)

    pl.semaphore_wait(barrier, chips + jnp.minimum(sp, 1) + jnp.minimum(s - 1 - sp, 1))

    up = {"space": sp + 1}
    down = {"space": sp - 1}
    to_up = [
        pltpu.make_async_remote_copy(
            ext.at[pl.ds(rows, HALO)], ext.at[pl.ds(0, HALO)],
            halo_send.at[0], halo_recv.at[0], device_id=up,
        ),
        pltpu.make_async_remote_copy(
            mask_s.at[pl.ds(rows, HALO)], mask_s.at[pl.ds(0, HALO)],
            halo_send.at[1], halo_recv.at[1], device_id=up,
        ),
    ]
    to_down = [
        pltpu.make_async_remote_copy(
            ext.at[pl.ds(HALO, HALO)], ext.at[pl.ds(rows + HALO, HALO)],
            halo_send.at[2], halo_recv.at[2], device_id=down,
        ),
        pltpu.make_async_remote_copy(
            mask_s.at[pl.ds(HALO, HALO)], mask_s.at[pl.ds(rows + HALO, HALO)],
            halo_send.at[3], halo_recv.at[3], device_id=down,
        ),
    ]

    @pl.when(sp > 0)
    def _():
        for copy in to_down:
            copy.start()

    @pl.when(sp == 0)
    def _():
        ext[pl.ds(0, HALO)] = jnp.zeros((HALO, nb, cols), jnp.float32)
        mask_s[pl.ds(0, HALO)] = jnp.zeros((HALO, 1, cols), jnp.float32)

    @pl.when(sp == s - 1)
    def _():
        ext[pl.ds(rows + HALO, HALO)] = jnp.zeros((HALO, nb, cols), jnp.float32)
        mask_s[pl.ds(rows + HALO, HALO)] = jnp.zeros((HALO, 1, cols), jnp.float32)

    def start_row(j):
        return lax.rem(j * UNIT + CHUNK, rows)

    def block(j, owner):
        return every.at[
            pl.ds(start_row(j), UNIT), pl.ds(pl.multiple_of(owner * nb, 16), nb)
        ]

    def far_copy(j, k, owner):
        part = block(j, owner)
        return pltpu.make_async_remote_copy(
            part, part, x_send.at[j, k], x_recv.at[j, k], device_id={"bin": far_to(k)}
        )

    def near_copy(j, k, owner):
        part = block(j, owner)
        return pltpu.make_async_remote_copy(
            part, part, f_send.at[j, k], f_recv.at[j, k], device_id={"bin": sibling}
        )

    def other(owner):
        return owner + 1 - 2 * core

    tab_load.wait()
    lane = lax.broadcasted_iota(jnp.int32, (8, cols), 1)

    def propagate(t):
        base = t * TILE

        def group(g, carry):
            at = pl.multiple_of(g * 8, 8)
            coef = tab[pl.ds(at, 8)]

            def wide(col):
                return jnp.broadcast_to(coef[:, col : col + 1], (8, cols))

            ax, ay = wide(AX), wide(AY)
            xpos, ypos = wide(XPOS) > 0.5, wide(YPOS) > 0.5
            edge = jnp.where(
                jnp.where(ypos, lane, cols - 1 - lane) == 0, 0.0, 1.0
            )
            field = [ext[base + m, pl.ds(at, 8)] for m in range(TILE + 2 * HALO)]
            for step in range(3):
                new = []
                for m in range(1, len(field) - 1):
                    e = field[m]
                    back = jnp.where(xpos, field[m - 1], field[m + 1])
                    side = edge * jnp.where(
                        ypos, pltpu.roll(e, 1, 1), pltpu.roll(e, cols - 1, 1)
                    )
                    value = e - ax * (e - back) - ay * (e - side)
                    new.append(value * mask_s[base + m + step])
                field = new
            where = pl.multiple_of(b * nb + at, 8)
            for m in range(TILE):
                every[base + m, pl.ds(where, 8)] = field[m]
            return carry

        lax.fori_loop(0, nb // 8, group, 0)

    def tile_step(i, carry):
        t = lax.rem(i + CHUNK // TILE, tiles)

        for c in range(2, chunks):

            @pl.when(i == (c * CHUNK - HALO - CHUNK) // TILE)
            def _():
                loads[c].wait()
                to_rows(c)

        @pl.when(i == (rows - CHUNK - HALO - CHUNK) // TILE)
        def _():
            @pl.when(sp < s - 1)
            def _():
                for copy in to_up:
                    copy.start()

        @pl.when(i == (rows - HALO - CHUNK) // TILE)
        def _():
            @pl.when(sp > 0)
            def _():
                for copy in to_up:
                    copy.wait_recv()

            @pl.when(sp < s - 1)
            def _():
                for copy in to_down:
                    copy.wait_recv()

        propagate(t)

        def send(p, carry):
            j = i * (TILE // UNIT) + p
            for k in range(1, chips):
                far_copy(j, k, b).start()
            near_copy(j, 0, b).start()
            return carry

        lax.fori_loop(0, TILE // UNIT, send, 0)
        return carry

    lax.fori_loop(0, tiles, tile_step, 0)

    @pl.when(sp < s - 1)
    def _():
        for copy in to_up:
            copy.wait_send()

    @pl.when(sp > 0)
    def _():
        for copy in to_down:
            copy.wait_send()

    u_all = 0.77 * speed[...] * jnp.cos(heading[...])
    v_all = 0.77 * speed[...] * jnp.sin(heading[...])
    for r in range(rows):
        u_s[r] = u_all[r : r + 1]
        v_s[r] = v_all[r : r + 1]

    q_load.wait()
    turned = jnp.dot(
        reversal(nb, 0, nb, 0), q2[pl.ds(0, nb)], preferred_element_type=jnp.float32
    ).astype(jnp.bfloat16)
    for c in range(BINS // 256):
        q2[pl.ds(nb, nb), pl.ds(c * 256, 256)] = jnp.dot(
            turned, reversal(BINS, 0, 256, c * 256), preferred_element_type=jnp.float32
        ).astype(jnp.bfloat16)

    own = pl.ds(pl.multiple_of(b * nb, 16), nb)

    def compute(row):
        total = jnp.sum(every[row], axis=0, keepdims=True) * (1.0 / BINS)
        low = every[row].astype(jnp.bfloat16)
        coupled = jnp.dot(q2[...], low, preferred_element_type=jnp.float32)
        energy = every[row, own]
        along = tab[:, FCOS : FCOS + 1] * u_s[row] + tab[:, FSIN : FSIN + 1] * v_s[row]
        growth = GROWTH * jnp.maximum(along - 1.0, 0.0)
        rate = (
            growth
            + NONLINEAR * (coupled[:nb] + coupled[nb:])
            - DAMPING * tab[:, STEEP2 : STEEP2 + 1] * (total * total)
        )
        ext[HALO + row] = energy + TIME_STEP * (rate * energy)

    def out_copy(c):
        return pltpu.make_async_copy(
            nat.at[c], out.at[:, pl.ds(pl.multiple_of(c * CHUNK, CHUNK), CHUNK)], out_sem.at[c]
        )

    def unit_step(j, carry):
        @pl.when(j < units)
        def _():
            for k in range(1, chips):
                far_copy(j, k, far_from(k)).wait_recv()
                near_copy(j, k, far_from(k)).start()

        @pl.when(j > 0)
        def _():
            near_copy(j - 1, 0, sibling).wait_recv()
            for k in range(1, chips):
                near_copy(j - 1, k, other(far_from(k))).wait_recv()
            for r in range(UNIT):
                compute(start_row(j - 1) + r)

            @pl.when(lax.rem(j * UNIT, CHUNK) == 0)
            def _():
                c = start_row(j - 1) // CHUNK
                to_bins(c)
                out_copy(c).start()

        return carry

    lax.fori_loop(0, units + 1, unit_step, 0)

    def drain(j, carry):
        for k in range(1, chips):
            far_copy(j, k, b).wait_send()
            near_copy(j, k, far_from(k)).wait_send()
        near_copy(j, 0, b).wait_send()
        return carry

    lax.fori_loop(0, units, drain, 0)
    for c in range(chunks):
        out_copy(c).wait()


def on_device(n, s, spectrum, sea_mask, wind_speed, wind_heading, quad):
    nb, rows, cols = spectrum.shape
    units, chips, chunks = rows // UNIT, n // 2, rows // CHUNK
    vmem = pl.BlockSpec(memory_space=pltpu.VMEM)
    hbm = pl.BlockSpec(memory_space=pl.ANY)
    return pl.pallas_call(
        functools.partial(kernel, n, s),
        out_shape=jax.ShapeDtypeStruct((nb, rows, cols), jnp.float32),
        in_specs=[hbm, vmem, vmem, vmem, hbm, hbm],
        out_specs=hbm,
        scratch_shapes=[
            pltpu.VMEM((chunks, nb, CHUNK, cols), jnp.float32),
            pltpu.VMEM((rows + 2 * HALO, nb, cols), jnp.float32),
            pltpu.VMEM((rows + 2 * HALO, 1, cols), jnp.float32),
            pltpu.VMEM((rows, 1, cols), jnp.float32),
            pltpu.VMEM((rows, 1, cols), jnp.float32),
            pltpu.VMEM((rows, BINS, cols), jnp.float32),
            pltpu.VMEM((2 * nb, BINS), jnp.bfloat16),
            pltpu.VMEM((nb, 128), jnp.float32),
            pltpu.SemaphoreType.DMA((chunks + 2,)),
            pltpu.SemaphoreType.DMA((4,)),
            pltpu.SemaphoreType.DMA((4,)),
            pltpu.SemaphoreType.DMA((units, chips)),
            pltpu.SemaphoreType.DMA((units, chips)),
            pltpu.SemaphoreType.DMA((units, chips)),
            pltpu.SemaphoreType.DMA((units, chips)),
            pltpu.SemaphoreType.DMA((chunks,)),
        ],
        compiler_params=pltpu.CompilerParams(
            collective_id=0, has_side_effects=True, vmem_limit_bytes=53 * 1024 * 1024
        ),
        cost_estimate=pl.CostEstimate(
            flops=4 * nb * BINS * rows * cols, bytes_accessed=8 * nb * rows * cols, transcendentals=0
        ),
        name="wave_step",
    )(
        spectrum, sea_mask, wind_speed, wind_heading, quad, jnp.asarray(bin_tables()),
    )


def solution(mesh):
    return jax.shard_map(
        functools.partial(on_device, mesh.shape["bin"], mesh.shape["space"]),
        mesh=mesh,
        in_specs=(
            P("bin", "space", None),
            P("space", None),
            P("space", None),
            P("space", None),
            P(),
        ),
        out_specs=P("bin", "space", None),
        check_vma=False,
    )
```

```python
import functools
import math

import jax
import jax.numpy as jnp
import numpy as np
from jax import lax
from jax.experimental import pallas as pl
from jax.experimental.pallas import tpu as pltpu
from jax.sharding import PartitionSpec as P

FREQS = 32
DIRS = 24
BINS = 768

LOG_RATIO = math.log(1.1)
TWO_PI = 2.0 * math.pi
TIME_STEP = 0.2
NONLINEAR = 1.5
DAMPING = 2.0
GROWTH = 0.15

HALO = 3
CHUNK = 8
TILE = 2
UNIT = 2

AX, AY, XPOS, YPOS, FCOS, FSIN, STEEP2 = range(7)


def bin_tables():
    bins = np.arange(BINS)
    level = (bins // DIRS).astype(np.float64)
    direction = (bins % DIRS).astype(np.float64)
    frequency = 0.04 * np.exp(level * LOG_RATIO)
    courant = 0.65 * np.exp(-level * LOG_RATIO)
    theta = (direction + 0.5) * (TWO_PI / DIRS)
    cos_theta, sin_theta = np.cos(theta), np.sin(theta)
    top_freq = 0.04 * math.exp((FREQS - 1) * LOG_RATIO)
    table = np.zeros((BINS, 128), np.float32)
    table[:, AX] = np.abs(courant * cos_theta)
    table[:, AY] = np.abs(courant * sin_theta)
    table[:, XPOS] = cos_theta > 0
    table[:, YPOS] = sin_theta > 0
    table[:, FCOS] = frequency * cos_theta
    table[:, FSIN] = frequency * sin_theta
    table[:, STEEP2] = (frequency / top_freq) ** 2
    return table


def reversal(rows, row_start, cols, col_start):
    i = lax.broadcasted_iota(jnp.int32, (rows, cols), 0).astype(jnp.float32) + row_start
    j = lax.broadcasted_iota(jnp.int32, (rows, cols), 1).astype(jnp.float32) + col_start
    level = jnp.floor((i + 0.5) * (1.0 / DIRS))
    return jnp.where(i + j == 2 * DIRS * level + (DIRS - 1), 1.0, 0.0).astype(jnp.bfloat16)


def kernel(
    n, s, spec, mask_h, speed_h, heading_h, quad, table, nat,
    mask, speed, heading, ext, mask_s, u_s, v_s, every, q2, tab,
    load_sem, small_sem, halo_send, halo_recv, x_send, x_recv, f_send, f_recv,
):
    nb, rows, cols = spec.shape
    tiles = rows // TILE
    chunks = rows // CHUNK
    units = rows // UNIT
    chips = n // 2
    b = lax.axis_index("bin")
    sp = lax.axis_index("space")
    chip, core = b // 2, lax.rem(b, 2)
    sibling = chip * 2 + 1 - core

    def far_to(k):
        return lax.rem(chip + k, chips) * 2 + core

    def far_from(k):
        return lax.rem(chip + chips - k, chips) * 2 + core

    loads = [
        pltpu.make_async_copy(
            spec.at[:, pl.ds(c * CHUNK, CHUNK)], nat.at[:, pl.ds(c * CHUNK, CHUNK)],
            load_sem.at[c],
        )
        for c in range(chunks)
    ]
    smalls = [
        pltpu.make_async_copy(source, target, small_sem.at[at])
        for at, (source, target) in enumerate(
            ((mask_h, mask), (speed_h, speed), (heading_h, heading))
        )
    ]
    loads[0].start()
    smalls[0].start()
    for load in loads[1:]:
        load.start()
    for small in smalls[1:]:
        small.start()
    tab_load = pltpu.make_async_copy(
        table.at[pl.ds(pl.multiple_of(b * nb, 16), nb)], tab, load_sem.at[chunks]
    )
    tab_load.start()
    q_load = pltpu.make_async_copy(
        quad.at[pl.ds(pl.multiple_of(b * nb, 16), nb)], q2.at[pl.ds(0, nb)], load_sem.at[chunks + 1]
    )
    q_load.start()

    barrier = pltpu.get_barrier_semaphore()
    pl.semaphore_signal(barrier, 1, device_id={"bin": sibling})
    for k in range(1, chips):
        pl.semaphore_signal(barrier, 1, device_id={"bin": far_to(k)})

    @pl.when(sp > 0)
    def _():
        pl.semaphore_signal(barrier, 1, device_id={"space": sp - 1})

    @pl.when(sp < s - 1)
    def _():
        pl.semaphore_signal(barrier, 1, device_id={"space": sp + 1})

    smalls[0].wait()
    mask_f = mask[...].astype(jnp.float32)
    for r in range(rows):
        mask_s[HALO + r] = mask_f[r : r + 1]

    def to_rows(c):
        def group(g, carry):
            at = pl.ds(pl.multiple_of(g * 8, 8), 8)
            ext[pl.ds(HALO + c * CHUNK, CHUNK), at] = jnp.swapaxes(
                nat[at, pl.ds(c * CHUNK, CHUNK)], 0, 1
            )
            return carry

        lax.fori_loop(0, nb // 8, group, 0)

    def to_bins(c):
        def group(g, carry):
            at = pl.ds(pl.multiple_of(g * 8, 8), 8)
            nat[at, pl.ds(pl.multiple_of(c * CHUNK, CHUNK), CHUNK)] = jnp.swapaxes(
                ext[pl.ds(HALO + c * CHUNK, CHUNK), at], 0, 1
            )
            return carry

        lax.fori_loop(0, nb // 8, group, 0)

    for c in range(2):
        loads[c].wait()
        to_rows(c)

    pl.semaphore_wait(barrier, chips + jnp.minimum(sp, 1) + jnp.minimum(s - 1 - sp, 1))

    up = {"space": sp + 1}
    down = {"space": sp - 1}
    to_up = [
        pltpu.make_async_remote_copy(
            ext.at[pl.ds(rows, HALO)], ext.at[pl.ds(0, HALO)],
            halo_send.at[0], halo_recv.at[0], device_id=up,
        ),
        pltpu.make_async_remote_copy(
            mask_s.at[pl.ds(rows, HALO)], mask_s.at[pl.ds(0, HALO)],
            halo_send.at[1], halo_recv.at[1], device_id=up,
        ),
    ]
    to_down = [
        pltpu.make_async_remote_copy(
            ext.at[pl.ds(HALO, HALO)], ext.at[pl.ds(rows + HALO, HALO)],
            halo_send.at[2], halo_recv.at[2], device_id=down,
        ),
        pltpu.make_async_remote_copy(
            mask_s.at[pl.ds(HALO, HALO)], mask_s.at[pl.ds(rows + HALO, HALO)],
            halo_send.at[3], halo_recv.at[3], device_id=down,
        ),
    ]

    @pl.when(sp > 0)
    def _():
        for copy in to_down:
            copy.start()

    @pl.when(sp == 0)
    def _():
        ext[pl.ds(0, HALO)] = jnp.zeros((HALO, nb, cols), jnp.float32)
        mask_s[pl.ds(0, HALO)] = jnp.zeros((HALO, 1, cols), jnp.float32)

    @pl.when(sp == s - 1)
    def _():
        ext[pl.ds(rows + HALO, HALO)] = jnp.zeros((HALO, nb, cols), jnp.float32)
        mask_s[pl.ds(rows + HALO, HALO)] = jnp.zeros((HALO, 1, cols), jnp.float32)

    def start_row(j):
        return lax.rem(j * UNIT + CHUNK, rows)

    def block(j, owner):
        return every.at[
            pl.ds(start_row(j), UNIT), pl.ds(pl.multiple_of(owner * nb, 16), nb)
        ]

    def far_copy(j, k, owner):
        part = block(j, owner)
        return pltpu.make_async_remote_copy(
            part, part, x_send.at[j, k], x_recv.at[j, k], device_id={"bin": far_to(k)}
        )

    def near_copy(j, k, owner):
        part = block(j, owner)
        return pltpu.make_async_remote_copy(
            part, part, f_send.at[j, k], f_recv.at[j, k], device_id={"bin": sibling}
        )

    def other(owner):
        return owner + 1 - 2 * core

    tab_load.wait()
    lane = lax.broadcasted_iota(jnp.int32, (8, cols), 1)

    def propagate(t):
        base = t * TILE

        def group(g, carry):
            at = pl.multiple_of(g * 8, 8)
            coef = tab[pl.ds(at, 8)]

            def wide(col):
                return jnp.broadcast_to(coef[:, col : col + 1], (8, cols))

            ax, ay = wide(AX), wide(AY)
            xpos, ypos = wide(XPOS) > 0.5, wide(YPOS) > 0.5
            edge = jnp.where(
                jnp.where(ypos, lane, cols - 1 - lane) == 0, 0.0, 1.0
            )
            field = [ext[base + m, pl.ds(at, 8)] for m in range(TILE + 2 * HALO)]
            for step in range(3):
                new = []
                for m in range(1, len(field) - 1):
                    e = field[m]
                    back = jnp.where(xpos, field[m - 1], field[m + 1])
                    side = edge * jnp.where(
                        ypos, pltpu.roll(e, 1, 1), pltpu.roll(e, cols - 1, 1)
                    )
                    value = e - ax * (e - back) - ay * (e - side)
                    new.append(value * mask_s[base + m + step])
                field = new
            where = pl.multiple_of(b * nb + at, 8)
            for m in range(TILE):
                every[base + m, pl.ds(where, 8)] = field[m]
            return carry

        lax.fori_loop(0, nb // 8, group, 0)

    def tile_step(i, carry):
        t = lax.rem(i + CHUNK // TILE, tiles)

        for c in range(2, chunks):

            @pl.when(i == (c * CHUNK - HALO - CHUNK) // TILE)
            def _():
                loads[c].wait()
                to_rows(c)

        @pl.when(i == (rows - CHUNK - HALO - CHUNK) // TILE)
        def _():
            @pl.when(sp < s - 1)
            def _():
                for copy in to_up:
                    copy.start()

        @pl.when(i == (rows - HALO - CHUNK) // TILE)
        def _():
            @pl.when(sp > 0)
            def _():
                for copy in to_up:
                    copy.wait_recv()

            @pl.when(sp < s - 1)
            def _():
                for copy in to_down:
                    copy.wait_recv()

        propagate(t)

        def send(p, carry):
            j = i * (TILE // UNIT) + p
            for k in range(1, chips):
                far_copy(j, k, b).start()
            near_copy(j, 0, b).start()
            return carry

        lax.fori_loop(0, TILE // UNIT, send, 0)
        return carry

    lax.fori_loop(0, tiles, tile_step, 0)

    @pl.when(sp < s - 1)
    def _():
        for copy in to_up:
            copy.wait_send()

    @pl.when(sp > 0)
    def _():
        for copy in to_down:
            copy.wait_send()

    for small in smalls[1:]:
        small.wait()
    u_all = 0.77 * speed[...] * jnp.cos(heading[...])
    v_all = 0.77 * speed[...] * jnp.sin(heading[...])
    for r in range(rows):
        u_s[r] = u_all[r : r + 1]
        v_s[r] = v_all[r : r + 1]

    q_load.wait()
    turned = jnp.dot(
        reversal(nb, 0, nb, 0), q2[pl.ds(0, nb)], preferred_element_type=jnp.float32
    ).astype(jnp.bfloat16)
    for c in range(BINS // 256):
        q2[pl.ds(nb, nb), pl.ds(c * 256, 256)] = jnp.dot(
            turned, reversal(BINS, 0, 256, c * 256), preferred_element_type=jnp.float32
        ).astype(jnp.bfloat16)

    own = pl.ds(pl.multiple_of(b * nb, 16), nb)

    def compute(row):
        total = jnp.sum(every[row], axis=0, keepdims=True) * (1.0 / BINS)
        low = every[row].astype(jnp.bfloat16)
        coupled = jnp.dot(q2[...], low, preferred_element_type=jnp.float32)
        energy = every[row, own]
        along = tab[:, FCOS : FCOS + 1] * u_s[row] + tab[:, FSIN : FSIN + 1] * v_s[row]
        growth = GROWTH * jnp.maximum(along - 1.0, 0.0)
        rate = (
            growth
            + NONLINEAR * (coupled[:nb] + coupled[nb:])
            - DAMPING * tab[:, STEEP2 : STEEP2 + 1] * (total * total)
        )
        ext[HALO + row] = energy + TIME_STEP * (rate * energy)

    def unit_step(j, carry):
        @pl.when(j < units)
        def _():
            for k in range(1, chips):
                far_copy(j, k, far_from(k)).wait_recv()
                near_copy(j, k, far_from(k)).start()

        @pl.when(j > 0)
        def _():
            near_copy(j - 1, 0, sibling).wait_recv()
            for k in range(1, chips):
                near_copy(j - 1, k, other(far_from(k))).wait_recv()
            for r in range(UNIT):
                compute(start_row(j - 1) + r)

            @pl.when(lax.rem(j * UNIT, CHUNK) == 0)
            def _():
                to_bins(start_row(j - 1) // CHUNK)

        return carry

    lax.fori_loop(0, units + 1, unit_step, 0)

    def drain(j, carry):
        for k in range(1, chips):
            far_copy(j, k, b).wait_send()
            near_copy(j, k, far_from(k)).wait_send()
        near_copy(j, 0, b).wait_send()
        return carry

    lax.fori_loop(0, units, drain, 0)


def on_device(n, s, spectrum, sea_mask, wind_speed, wind_heading, quad):
    nb, rows, cols = spectrum.shape
    units, chips, chunks = rows // UNIT, n // 2, rows // CHUNK
    vmem = pl.BlockSpec(memory_space=pltpu.VMEM)
    hbm = pl.BlockSpec(memory_space=pl.ANY)
    return pl.pallas_call(
        functools.partial(kernel, n, s),
        out_shape=pltpu.VMEM((nb, rows, cols), jnp.float32),
        in_specs=[hbm] * 6,
        out_specs=vmem,
        scratch_shapes=[
            pltpu.VMEM((rows, cols), jnp.int32),
            pltpu.VMEM((rows, cols), jnp.float32),
            pltpu.VMEM((rows, cols), jnp.float32),
            pltpu.VMEM((rows + 2 * HALO, nb, cols), jnp.float32),
            pltpu.VMEM((rows + 2 * HALO, 1, cols), jnp.float32),
            pltpu.VMEM((rows, 1, cols), jnp.float32),
            pltpu.VMEM((rows, 1, cols), jnp.float32),
            pltpu.VMEM((rows, BINS, cols), jnp.float32),
            pltpu.VMEM((2 * nb, BINS), jnp.bfloat16),
            pltpu.VMEM((nb, 128), jnp.float32),
            pltpu.SemaphoreType.DMA((chunks + 2,)),
            pltpu.SemaphoreType.DMA((3,)),
            pltpu.SemaphoreType.DMA((4,)),
            pltpu.SemaphoreType.DMA((4,)),
            pltpu.SemaphoreType.DMA((units, chips)),
            pltpu.SemaphoreType.DMA((units, chips)),
            pltpu.SemaphoreType.DMA((units, chips)),
            pltpu.SemaphoreType.DMA((units, chips)),
        ],
        compiler_params=pltpu.CompilerParams(
            collective_id=0, has_side_effects=True, vmem_limit_bytes=56 * 1024 * 1024
        ),
        cost_estimate=pl.CostEstimate(
            flops=4 * nb * BINS * rows * cols, bytes_accessed=8 * nb * rows * cols, transcendentals=0
        ),
        name="wave_step",
    )(
        spectrum, sea_mask, wind_speed, wind_heading, quad, jnp.asarray(bin_tables()),
    )


def solution(mesh):
    return jax.shard_map(
        functools.partial(on_device, mesh.shape["bin"], mesh.shape["space"]),
        mesh=mesh,
        in_specs=(
            P("bin", "space", None),
            P("space", None),
            P("space", None),
            P("space", None),
            P(),
        ),
        out_specs=P("bin", "space", None),
        check_vma=False,
    )
```

```python
import functools
import math

import jax
import jax.numpy as jnp
import numpy as np
from jax import lax
from jax.experimental import pallas as pl
from jax.experimental.pallas import tpu as pltpu
from jax.sharding import PartitionSpec as P

FREQS = 32
DIRS = 24
BINS = 768

LOG_RATIO = math.log(1.1)
TWO_PI = 2.0 * math.pi
TIME_STEP = 0.2
NONLINEAR = 1.5
DAMPING = 2.0
GROWTH = 0.15

HALO = 3
CHUNK = 8
TILE = 2
UNIT = 2

AX, AY, XPOS, YPOS, FCOS, FSIN, STEEP2 = range(7)


def bin_tables():
    bins = np.arange(BINS)
    level = (bins // DIRS).astype(np.float64)
    direction = (bins % DIRS).astype(np.float64)
    frequency = 0.04 * np.exp(level * LOG_RATIO)
    courant = 0.65 * np.exp(-level * LOG_RATIO)
    theta = (direction + 0.5) * (TWO_PI / DIRS)
    cos_theta, sin_theta = np.cos(theta), np.sin(theta)
    top_freq = 0.04 * math.exp((FREQS - 1) * LOG_RATIO)
    table = np.zeros((BINS, 128), np.float32)
    table[:, AX] = np.abs(courant * cos_theta)
    table[:, AY] = np.abs(courant * sin_theta)
    table[:, XPOS] = cos_theta > 0
    table[:, YPOS] = sin_theta > 0
    table[:, FCOS] = frequency * cos_theta
    table[:, FSIN] = frequency * sin_theta
    table[:, STEEP2] = (frequency / top_freq) ** 2
    return table


def reversal(rows, row_start, cols, col_start):
    i = lax.broadcasted_iota(jnp.int32, (rows, cols), 0).astype(jnp.float32) + row_start
    j = lax.broadcasted_iota(jnp.int32, (rows, cols), 1).astype(jnp.float32) + col_start
    level = jnp.floor((i + 0.5) * (1.0 / DIRS))
    return jnp.where(i + j == 2 * DIRS * level + (DIRS - 1), 1.0, 0.0).astype(jnp.bfloat16)


def part_count(nb):
    return 4 if nb % 32 == 0 else 2


def kernel(
    n, s, spec, mask_h, speed_h, heading_h, quad, table, nat,
    mask, speed, heading, ext, mask_s, u_s, v_s, every, q2, tab,
    load_sem, first_sem, small_sem, halo_send, halo_recv, x_send, x_recv, f_send, f_recv, part_send, part_recv,
):
    nb, rows, cols = spec.shape
    tiles = rows // TILE
    chunks = rows // CHUNK
    parts = part_count(nb)
    width = nb // parts
    units = rows // UNIT
    chips = n // 2
    b = lax.axis_index("bin")
    sp = lax.axis_index("space")
    chip, core = b // 2, lax.rem(b, 2)
    sibling = chip * 2 + 1 - core

    def far_to(k):
        return lax.rem(chip + k, chips) * 2 + core

    def far_from(k):
        return lax.rem(chip + chips - k, chips) * 2 + core

    loads = [
        pltpu.make_async_copy(
            spec.at[:, pl.ds(c * CHUNK, CHUNK)], nat.at[:, pl.ds(c * CHUNK, CHUNK)],
            load_sem.at[c],
        )
        for c in range(2, chunks)
    ]
    firsts = [
        pltpu.make_async_copy(
            spec.at[pl.ds(q * width, width), pl.ds(0, 2 * CHUNK)],
            nat.at[pl.ds(q * width, width), pl.ds(0, 2 * CHUNK)],
            first_sem.at[q],
        )
        for q in range(parts)
    ]
    smalls = [
        pltpu.make_async_copy(source, target, small_sem.at[at])
        for at, (source, target) in enumerate(
            ((mask_h, mask), (speed_h, speed), (heading_h, heading))
        )
    ]
    firsts[0].start()
    smalls[0].start()
    for small in smalls[1:]:
        small.start()
    tab_load = pltpu.make_async_copy(
        table.at[pl.ds(pl.multiple_of(b * nb, 16), nb)], tab, load_sem.at[chunks]
    )
    tab_load.start()
    for load in firsts[1:] + loads:
        load.start()
    q_load = pltpu.make_async_copy(
        quad.at[pl.ds(pl.multiple_of(b * nb, 16), nb)], q2.at[pl.ds(0, nb)], load_sem.at[chunks + 1]
    )
    q_load.start()

    barrier = pltpu.get_barrier_semaphore()
    pl.semaphore_signal(barrier, 1, device_id={"bin": sibling})
    for k in range(1, chips):
        pl.semaphore_signal(barrier, 1, device_id={"bin": far_to(k)})

    @pl.when(sp > 0)
    def _():
        pl.semaphore_signal(barrier, 1, device_id={"space": sp - 1})

    @pl.when(sp < s - 1)
    def _():
        pl.semaphore_signal(barrier, 1, device_id={"space": sp + 1})

    smalls[0].wait()
    mask_f = mask[...].astype(jnp.float32)
    for r in range(rows):
        mask_s[HALO + r] = mask_f[r : r + 1]

    def to_rows(c, first=0, last=nb // 8):
        def group(g, carry):
            at = pl.ds(pl.multiple_of(g * 8, 8), 8)
            ext[pl.ds(HALO + c * CHUNK, CHUNK), at] = jnp.swapaxes(
                nat[at, pl.ds(c * CHUNK, CHUNK)], 0, 1
            )
            return carry

        lax.fori_loop(first, last, group, 0)

    def to_bins(c):
        def group(g, carry):
            at = pl.ds(pl.multiple_of(g * 8, 8), 8)
            nat[at, pl.ds(pl.multiple_of(c * CHUNK, CHUNK), CHUNK)] = jnp.swapaxes(
                ext[pl.ds(HALO + c * CHUNK, CHUNK), at], 0, 1
            )
            return carry

        lax.fori_loop(0, nb // 8, group, 0)

    up = {"space": sp + 1}
    down = {"space": sp - 1}
    to_up = [
        pltpu.make_async_remote_copy(
            ext.at[pl.ds(rows, HALO)], ext.at[pl.ds(0, HALO)],
            halo_send.at[0], halo_recv.at[0], device_id=up,
        ),
        pltpu.make_async_remote_copy(
            mask_s.at[pl.ds(rows, HALO)], mask_s.at[pl.ds(0, HALO)],
            halo_send.at[1], halo_recv.at[1], device_id=up,
        ),
    ]
    to_down = [
        pltpu.make_async_remote_copy(
            ext.at[pl.ds(HALO, HALO)], ext.at[pl.ds(rows + HALO, HALO)],
            halo_send.at[2], halo_recv.at[2], device_id=down,
        ),
        pltpu.make_async_remote_copy(
            mask_s.at[pl.ds(HALO, HALO)], mask_s.at[pl.ds(rows + HALO, HALO)],
            halo_send.at[3], halo_recv.at[3], device_id=down,
        ),
    ]

    def start_row(j):
        return lax.rem(j * UNIT + CHUNK, rows)

    last = units - 1
    last_row = (last * UNIT + CHUNK) % rows

    def block(row, count, owner):
        return every.at[pl.ds(row, count), pl.ds(pl.multiple_of(owner * nb, 16), nb)]

    def far_piece(row, count, j, k, owner):
        part = block(row, count, owner)
        return pltpu.make_async_remote_copy(
            part, part, x_send.at[j, k], x_recv.at[j, k], device_id={"bin": far_to(k)}
        )

    def near_piece(row, count, j, k, owner):
        part = block(row, count, owner)
        return pltpu.make_async_remote_copy(
            part, part, f_send.at[j, k], f_recv.at[j, k], device_id={"bin": sibling}
        )

    def far_copy(j, k, owner):
        return far_piece(start_row(j), UNIT, j, k, owner)

    def near_copy(j, k, owner):
        return near_piece(start_row(j), UNIT, j, k, owner)

    def far_last(r, k, owner):
        return far_piece(last_row + r, 1, last + r, k, owner)

    def near_last(r, k, owner):
        return near_piece(last_row + r, 1, last + r, k, owner)

    def far_part(q, k, owner):
        part = every.at[
            pl.ds(CHUNK, UNIT), pl.ds(pl.multiple_of(owner * nb + q * width, 8), width)
        ]
        return pltpu.make_async_remote_copy(
            part, part, part_send.at[q, k], part_recv.at[q, k], device_id={"bin": far_to(k)}
        )

    def other(owner):
        return owner + 1 - 2 * core

    tab_load.wait()
    lane = lax.broadcasted_iota(jnp.int32, (8, cols), 1)

    def propagate(t, first=0, last=nb // 8):
        base = t * TILE

        def group(g, carry):
            at = pl.multiple_of(g * 8, 8)
            coef = tab[pl.ds(at, 8)]

            def wide(col):
                return jnp.broadcast_to(coef[:, col : col + 1], (8, cols))

            ax, ay = wide(AX), wide(AY)
            xpos, ypos = wide(XPOS) > 0.5, wide(YPOS) > 0.5
            edge = jnp.where(
                jnp.where(ypos, lane, cols - 1 - lane) == 0, 0.0, 1.0
            )
            field = [ext[base + m, pl.ds(at, 8)] for m in range(TILE + 2 * HALO)]
            for step in range(3):
                new = []
                for m in range(1, len(field) - 1):
                    e = field[m]
                    back = jnp.where(xpos, field[m - 1], field[m + 1])
                    side = edge * jnp.where(
                        ypos, pltpu.roll(e, 1, 1), pltpu.roll(e, cols - 1, 1)
                    )
                    value = e - ax * (e - back) - ay * (e - side)
                    new.append(value * mask_s[base + m + step])
                field = new
            where = pl.multiple_of(b * nb + at, 8)
            for m in range(TILE):
                every[base + m, pl.ds(where, 8)] = field[m]
            return carry

        lax.fori_loop(first, last, group, 0)

    for q in range(parts):
        span = (q * width // 8, (q + 1) * width // 8)
        firsts[q].wait()
        for c in range(2):
            to_rows(c, *span)
        propagate(CHUNK // TILE, *span)
        if q == 0:
            pl.semaphore_wait(barrier, chips + jnp.minimum(sp, 1) + jnp.minimum(s - 1 - sp, 1))
        for k in range(1, chips):
            far_part(q, k, b).start()
    near_copy(0, 0, b).start()

    @pl.when(sp > 0)
    def _():
        for copy in to_down:
            copy.start()

    @pl.when(sp == 0)
    def _():
        ext[pl.ds(0, HALO)] = jnp.zeros((HALO, nb, cols), jnp.float32)
        mask_s[pl.ds(0, HALO)] = jnp.zeros((HALO, 1, cols), jnp.float32)

    @pl.when(sp == s - 1)
    def _():
        ext[pl.ds(rows + HALO, HALO)] = jnp.zeros((HALO, nb, cols), jnp.float32)
        mask_s[pl.ds(rows + HALO, HALO)] = jnp.zeros((HALO, 1, cols), jnp.float32)

    def tile_step(i, carry):
        t = lax.rem(i + CHUNK // TILE, tiles)

        for c in range(2, chunks):

            @pl.when(i == (c * CHUNK - HALO - CHUNK) // TILE)
            def _():
                loads[c - 2].wait()
                to_rows(c)

        @pl.when(i == (rows - CHUNK - HALO - CHUNK) // TILE)
        def _():
            @pl.when(sp < s - 1)
            def _():
                for copy in to_up:
                    copy.start()

        @pl.when(i == (rows - HALO - CHUNK) // TILE)
        def _():
            @pl.when(sp > 0)
            def _():
                for copy in to_up:
                    copy.wait_recv()

            @pl.when(sp < s - 1)
            def _():
                for copy in to_down:
                    copy.wait_recv()

        propagate(t)

        @pl.when(i < last)
        def _():
            for k in range(1, chips):
                far_copy(i, k, b).start()
            near_copy(i, 0, b).start()

        @pl.when(i == last)
        def _():
            for r in range(UNIT):
                for k in range(1, chips):
                    far_last(r, k, b).start()
                near_last(r, 0, b).start()

        return carry

    lax.fori_loop(1, tiles, tile_step, 0)

    @pl.when(sp < s - 1)
    def _():
        for copy in to_up:
            copy.wait_send()

    @pl.when(sp > 0)
    def _():
        for copy in to_down:
            copy.wait_send()

    for small in smalls[1:]:
        small.wait()
    u_all = 0.77 * speed[...] * jnp.cos(heading[...])
    v_all = 0.77 * speed[...] * jnp.sin(heading[...])
    for r in range(rows):
        u_s[r] = u_all[r : r + 1]
        v_s[r] = v_all[r : r + 1]

    q_load.wait()
    turned = jnp.dot(
        reversal(nb, 0, nb, 0), q2[pl.ds(0, nb)], preferred_element_type=jnp.float32
    ).astype(jnp.bfloat16)
    for c in range(BINS // 256):
        q2[pl.ds(nb, nb), pl.ds(c * 256, 256)] = jnp.dot(
            turned, reversal(BINS, 0, 256, c * 256), preferred_element_type=jnp.float32
        ).astype(jnp.bfloat16)

    own = pl.ds(pl.multiple_of(b * nb, 16), nb)

    def compute(row):
        total = jnp.sum(every[row], axis=0, keepdims=True) * (1.0 / BINS)
        low = every[row].astype(jnp.bfloat16)
        coupled = jnp.dot(q2[...], low, preferred_element_type=jnp.float32)
        energy = every[row, own]
        along = tab[:, FCOS : FCOS + 1] * u_s[row] + tab[:, FSIN : FSIN + 1] * v_s[row]
        growth = GROWTH * jnp.maximum(along - 1.0, 0.0)
        rate = (
            growth
            + NONLINEAR * (coupled[:nb] + coupled[nb:])
            - DAMPING * tab[:, STEEP2 : STEEP2 + 1] * (total * total)
        )
        ext[HALO + row] = energy + TIME_STEP * (rate * energy)

    def unit_step(j, carry):
        @pl.when(j == 0)
        def _():
            for k in range(1, chips):
                for q in range(parts):
                    far_part(q, k, far_from(k)).wait_recv()
                near_copy(j, k, far_from(k)).start()

        @pl.when(j > 0)
        def _():
            for k in range(1, chips):
                far_copy(j, k, far_from(k)).wait_recv()
                near_copy(j, k, far_from(k)).start()

        near_copy(j, 0, sibling).wait_recv()
        for k in range(1, chips):
            near_copy(j, k, other(far_from(k))).wait_recv()
        for r in range(UNIT):
            compute(start_row(j) + r)

        @pl.when(lax.rem((j + 1) * UNIT, CHUNK) == 0)
        def _():
            to_bins(start_row(j) // CHUNK)

        return carry

    lax.fori_loop(0, last, unit_step, 0)

    for r in range(UNIT):
        for k in range(1, chips):
            far_last(r, k, far_from(k)).wait_recv()
            near_last(r, k, far_from(k)).start()
        near_last(r, 0, sibling).wait_recv()
        for k in range(1, chips):
            near_last(r, k, other(far_from(k))).wait_recv()
        compute(last_row + r)
    to_bins(last_row // CHUNK)

    def drain(j, carry):
        @pl.when(j > 0)
        def _():
            for k in range(1, chips):
                far_copy(j, k, b).wait_send()

        for k in range(1, chips):
            near_copy(j, k, far_from(k)).wait_send()
        near_copy(j, 0, b).wait_send()
        return carry

    lax.fori_loop(0, last, drain, 0)
    for r in range(UNIT):
        for k in range(1, chips):
            far_last(r, k, b).wait_send()
            near_last(r, k, far_from(k)).wait_send()
        near_last(r, 0, b).wait_send()
    for q in range(parts):
        for k in range(1, chips):
            far_part(q, k, b).wait_send()


def on_device(n, s, spectrum, sea_mask, wind_speed, wind_heading, quad):
    nb, rows, cols = spectrum.shape
    units, chips, chunks = rows // UNIT, n // 2, rows // CHUNK
    vmem = pl.BlockSpec(memory_space=pltpu.VMEM)
    hbm = pl.BlockSpec(memory_space=pl.ANY)
    return pl.pallas_call(
        functools.partial(kernel, n, s),
        out_shape=pltpu.VMEM((nb, rows, cols), jnp.float32),
        in_specs=[hbm] * 6,
        out_specs=vmem,
        scratch_shapes=[
            pltpu.VMEM((rows, cols), jnp.int32),
            pltpu.VMEM((rows, cols), jnp.float32),
            pltpu.VMEM((rows, cols), jnp.float32),
            pltpu.VMEM((rows + 2 * HALO, nb, cols), jnp.float32),
            pltpu.VMEM((rows + 2 * HALO, 1, cols), jnp.float32),
            pltpu.VMEM((rows, 1, cols), jnp.float32),
            pltpu.VMEM((rows, 1, cols), jnp.float32),
            pltpu.VMEM((rows, BINS, cols), jnp.float32),
            pltpu.VMEM((2 * nb, BINS), jnp.bfloat16),
            pltpu.VMEM((nb, 128), jnp.float32),
            pltpu.SemaphoreType.DMA((chunks + 2,)),
            pltpu.SemaphoreType.DMA((part_count(nb),)),
            pltpu.SemaphoreType.DMA((3,)),
            pltpu.SemaphoreType.DMA((4,)),
            pltpu.SemaphoreType.DMA((4,)),
            pltpu.SemaphoreType.DMA((units - 1 + UNIT, chips)),
            pltpu.SemaphoreType.DMA((units - 1 + UNIT, chips)),
            pltpu.SemaphoreType.DMA((units - 1 + UNIT, chips)),
            pltpu.SemaphoreType.DMA((units - 1 + UNIT, chips)),
            pltpu.SemaphoreType.DMA((part_count(nb), chips)),
            pltpu.SemaphoreType.DMA((part_count(nb), chips)),
        ],
        compiler_params=pltpu.CompilerParams(
            collective_id=0, has_side_effects=True, vmem_limit_bytes=56 * 1024 * 1024
        ),
        cost_estimate=pl.CostEstimate(
            flops=4 * nb * BINS * rows * cols, bytes_accessed=8 * nb * rows * cols, transcendentals=0
        ),
        name="wave_step",
    )(
        spectrum, sea_mask, wind_speed, wind_heading, quad, jnp.asarray(bin_tables()),
    )


def solution(mesh):
    return jax.shard_map(
        functools.partial(on_device, mesh.shape["bin"], mesh.shape["space"]),
        mesh=mesh,
        in_specs=(
            P("bin", "space", None),
            P("space", None),
            P("space", None),
            P("space", None),
            P(),
        ),
        out_specs=P("bin", "space", None),
        check_vma=False,
    )
```

```python
import functools
import math

import jax
import jax.numpy as jnp
import numpy as np
from jax import lax
from jax.experimental import pallas as pl
from jax.experimental.pallas import tpu as pltpu
from jax.sharding import PartitionSpec as P

FREQS = 32
DIRS = 24
BINS = 768

LOG_RATIO = math.log(1.1)
TWO_PI = 2.0 * math.pi
TIME_STEP = 0.2
NONLINEAR = 1.5
DAMPING = 2.0
GROWTH = 0.15

HALO = 3
CHUNK = 8
TILE = 2
UNIT = 2

AX, AY, XPOS, YPOS, FCOS, FSIN, STEEP2 = range(7)


def bin_tables():
    bins = np.arange(BINS)
    level = (bins // DIRS).astype(np.float64)
    direction = (bins % DIRS).astype(np.float64)
    frequency = 0.04 * np.exp(level * LOG_RATIO)
    courant = 0.65 * np.exp(-level * LOG_RATIO)
    theta = (direction + 0.5) * (TWO_PI / DIRS)
    cos_theta, sin_theta = np.cos(theta), np.sin(theta)
    top_freq = 0.04 * math.exp((FREQS - 1) * LOG_RATIO)
    table = np.zeros((BINS, 128), np.float32)
    table[:, AX] = np.abs(courant * cos_theta)
    table[:, AY] = np.abs(courant * sin_theta)
    table[:, XPOS] = cos_theta > 0
    table[:, YPOS] = sin_theta > 0
    table[:, FCOS] = frequency * cos_theta
    table[:, FSIN] = frequency * sin_theta
    table[:, STEEP2] = (frequency / top_freq) ** 2
    return table


def reversal(rows, row_start, cols, col_start):
    i = lax.broadcasted_iota(jnp.int32, (rows, cols), 0).astype(jnp.float32) + row_start
    j = lax.broadcasted_iota(jnp.int32, (rows, cols), 1).astype(jnp.float32) + col_start
    level = jnp.floor((i + 0.5) * (1.0 / DIRS))
    return jnp.where(i + j == 2 * DIRS * level + (DIRS - 1), 1.0, 0.0).astype(jnp.bfloat16)


def part_count(nb):
    return 4 if nb % 32 == 0 else 2


def kernel(
    n, s, spec, mask_h, speed_h, heading_h, quad, table, nat,
    mask, speed, heading, ext, mask_s, u_s, v_s, every, q2, tab,
    load_sem, first_sem, small_sem, halo_send, halo_recv, x_send, x_recv, f_send, f_recv, part_send, part_recv,
):
    nb, rows, cols = spec.shape
    tiles = rows // TILE
    chunks = rows // CHUNK
    parts = part_count(nb)
    width = nb // parts
    units = rows // UNIT
    chips = n // 2
    b = lax.axis_index("bin")
    sp = lax.axis_index("space")
    chip, core = b // 2, lax.rem(b, 2)
    sibling = chip * 2 + 1 - core

    def far_to(k):
        return lax.rem(chip + k, chips) * 2 + core

    def far_from(k):
        return lax.rem(chip + chips - k, chips) * 2 + core

    loads = [
        pltpu.make_async_copy(
            spec.at[:, pl.ds(c * CHUNK, CHUNK)], nat.at[:, pl.ds(c * CHUNK, CHUNK)],
            load_sem.at[c],
        )
        for c in range(2, chunks)
    ]
    firsts = [
        pltpu.make_async_copy(
            spec.at[pl.ds(q * width, width), pl.ds(0, 2 * CHUNK)],
            nat.at[pl.ds(q * width, width), pl.ds(0, 2 * CHUNK)],
            first_sem.at[q],
        )
        for q in range(parts)
    ]
    smalls = [
        pltpu.make_async_copy(source, target, small_sem.at[at])
        for at, (source, target) in enumerate(
            ((mask_h, mask), (speed_h, speed), (heading_h, heading))
        )
    ]
    firsts[0].start()
    smalls[0].start()
    for small in smalls[1:]:
        small.start()
    tab_load = pltpu.make_async_copy(
        table.at[pl.ds(pl.multiple_of(b * nb, 16), nb)], tab, load_sem.at[chunks]
    )
    tab_load.start()
    for load in firsts[1:] + loads:
        load.start()
    q_load = pltpu.make_async_copy(
        quad.at[pl.ds(pl.multiple_of(b * nb, 16), nb)], q2.at[pl.ds(0, nb)], load_sem.at[chunks + 1]
    )
    q_load.start()

    barrier = pltpu.get_barrier_semaphore()
    pl.semaphore_signal(barrier, 1, device_id={"bin": sibling})
    for k in range(1, chips):
        pl.semaphore_signal(barrier, 1, device_id={"bin": far_to(k)})

    @pl.when(sp > 0)
    def _():
        pl.semaphore_signal(barrier, 1, device_id={"space": sp - 1})

    @pl.when(sp < s - 1)
    def _():
        pl.semaphore_signal(barrier, 1, device_id={"space": sp + 1})

    smalls[0].wait()
    mask_f = mask[...].astype(jnp.float32)
    for r in range(rows):
        mask_s[HALO + r] = mask_f[r : r + 1]

    def to_rows(c, first=0, last=nb // 8):
        def group(g, carry):
            at = pl.ds(pl.multiple_of(g * 8, 8), 8)
            ext[pl.ds(HALO + c * CHUNK, CHUNK), at] = jnp.swapaxes(
                nat[at, pl.ds(c * CHUNK, CHUNK)], 0, 1
            )
            return carry

        lax.fori_loop(first, last, group, 0)

    def to_bins(c):
        def group(g, carry):
            at = pl.ds(pl.multiple_of(g * 8, 8), 8)
            nat[at, pl.ds(pl.multiple_of(c * CHUNK, CHUNK), CHUNK)] = jnp.swapaxes(
                ext[pl.ds(HALO + c * CHUNK, CHUNK), at], 0, 1
            )
            return carry

        lax.fori_loop(0, nb // 8, group, 0)

    up = {"space": sp + 1}
    down = {"space": sp - 1}
    to_up = [
        pltpu.make_async_remote_copy(
            ext.at[pl.ds(rows, HALO)], ext.at[pl.ds(0, HALO)],
            halo_send.at[0], halo_recv.at[0], device_id=up,
        ),
        pltpu.make_async_remote_copy(
            mask_s.at[pl.ds(rows, HALO)], mask_s.at[pl.ds(0, HALO)],
            halo_send.at[1], halo_recv.at[1], device_id=up,
        ),
    ]
    to_down = [
        pltpu.make_async_remote_copy(
            ext.at[pl.ds(HALO, HALO)], ext.at[pl.ds(rows + HALO, HALO)],
            halo_send.at[2], halo_recv.at[2], device_id=down,
        ),
        pltpu.make_async_remote_copy(
            mask_s.at[pl.ds(HALO, HALO)], mask_s.at[pl.ds(rows + HALO, HALO)],
            halo_send.at[3], halo_recv.at[3], device_id=down,
        ),
    ]

    def start_row(j):
        return lax.rem(j * UNIT + CHUNK, rows)

    last = units - 1
    last_row = (last * UNIT + CHUNK) % rows

    def block(row, count, owner):
        return every.at[pl.ds(row, count), pl.ds(pl.multiple_of(owner * nb, 16), nb)]

    def far_piece(row, count, j, k, owner):
        part = block(row, count, owner)
        return pltpu.make_async_remote_copy(
            part, part, x_send.at[j, k], x_recv.at[j, k], device_id={"bin": far_to(k)}
        )

    def near_piece(row, count, j, k, owner):
        part = block(row, count, owner)
        return pltpu.make_async_remote_copy(
            part, part, f_send.at[j, k], f_recv.at[j, k], device_id={"bin": sibling}
        )

    def far_copy(j, k, owner):
        return far_piece(start_row(j), UNIT, j, k, owner)

    def far_pair(j, k, owner):
        return far_piece(start_row(j), 2 * UNIT, j, k, owner)

    def alone(j):
        return (j == 1) | (j == last - 1)

    def paired(j):
        return (j > 1) & (j < last - 1) & (lax.rem(j, 2) == 0)

    def near_copy(j, k, owner):
        return near_piece(start_row(j), UNIT, j, k, owner)

    def far_last(r, k, owner):
        return far_piece(last_row + r, 1, last + r, k, owner)

    def near_last(r, k, owner):
        return near_piece(last_row + r, 1, last + r, k, owner)

    def far_part(q, k, owner):
        part = every.at[
            pl.ds(CHUNK, UNIT), pl.ds(pl.multiple_of(owner * nb + q * width, 8), width)
        ]
        return pltpu.make_async_remote_copy(
            part, part, part_send.at[q, k], part_recv.at[q, k], device_id={"bin": far_to(k)}
        )

    def other(owner):
        return owner + 1 - 2 * core

    tab_load.wait()
    lane = lax.broadcasted_iota(jnp.int32, (8, cols), 1)

    def propagate(t, first=0, last=nb // 8):
        base = t * TILE

        def group(g, carry):
            at = pl.multiple_of(g * 8, 8)
            coef = tab[pl.ds(at, 8)]

            def wide(col):
                return jnp.broadcast_to(coef[:, col : col + 1], (8, cols))

            ax, ay = wide(AX), wide(AY)
            xpos, ypos = wide(XPOS) > 0.5, wide(YPOS) > 0.5
            edge = jnp.where(
                jnp.where(ypos, lane, cols - 1 - lane) == 0, 0.0, 1.0
            )
            field = [ext[base + m, pl.ds(at, 8)] for m in range(TILE + 2 * HALO)]
            for step in range(3):
                new = []
                for m in range(1, len(field) - 1):
                    e = field[m]
                    back = jnp.where(xpos, field[m - 1], field[m + 1])
                    side = edge * jnp.where(
                        ypos, pltpu.roll(e, 1, 1), pltpu.roll(e, cols - 1, 1)
                    )
                    value = e - ax * (e - back) - ay * (e - side)
                    new.append(value * mask_s[base + m + step])
                field = new
            where = pl.multiple_of(b * nb + at, 8)
            for m in range(TILE):
                every[base + m, pl.ds(where, 8)] = field[m]
            return carry

        lax.fori_loop(first, last, group, 0)

    for q in range(parts):
        span = (q * width // 8, (q + 1) * width // 8)
        firsts[q].wait()
        for c in range(2):
            to_rows(c, *span)
        propagate(CHUNK // TILE, *span)
        if q == 0:
            pl.semaphore_wait(barrier, chips + jnp.minimum(sp, 1) + jnp.minimum(s - 1 - sp, 1))
        for k in range(1, chips):
            far_part(q, k, b).start()
    near_copy(0, 0, b).start()

    @pl.when(sp > 0)
    def _():
        for copy in to_down:
            copy.start()

    @pl.when(sp == 0)
    def _():
        ext[pl.ds(0, HALO)] = jnp.zeros((HALO, nb, cols), jnp.float32)
        mask_s[pl.ds(0, HALO)] = jnp.zeros((HALO, 1, cols), jnp.float32)

    @pl.when(sp == s - 1)
    def _():
        ext[pl.ds(rows + HALO, HALO)] = jnp.zeros((HALO, nb, cols), jnp.float32)
        mask_s[pl.ds(rows + HALO, HALO)] = jnp.zeros((HALO, 1, cols), jnp.float32)

    def tile_step(i, carry):
        t = lax.rem(i + CHUNK // TILE, tiles)

        for c in range(2, chunks):

            @pl.when(i == (c * CHUNK - HALO - CHUNK) // TILE)
            def _():
                loads[c - 2].wait()
                to_rows(c)

        @pl.when(i == (rows - CHUNK - HALO - CHUNK) // TILE)
        def _():
            @pl.when(sp < s - 1)
            def _():
                for copy in to_up:
                    copy.start()

        @pl.when(i == (rows - HALO - CHUNK) // TILE)
        def _():
            @pl.when(sp > 0)
            def _():
                for copy in to_up:
                    copy.wait_recv()

            @pl.when(sp < s - 1)
            def _():
                for copy in to_down:
                    copy.wait_recv()

        propagate(t)

        @pl.when(alone(i))
        def _():
            for k in range(1, chips):
                far_copy(i, k, b).start()

        @pl.when(paired(i - 1))
        def _():
            for k in range(1, chips):
                far_pair(i - 1, k, b).start()

        @pl.when(i < last)
        def _():
            near_copy(i, 0, b).start()

        @pl.when(i == last)
        def _():
            for r in range(UNIT):
                for k in range(1, chips):
                    far_last(r, k, b).start()
                near_last(r, 0, b).start()

        return carry

    lax.fori_loop(1, tiles, tile_step, 0)

    @pl.when(sp < s - 1)
    def _():
        for copy in to_up:
            copy.wait_send()

    @pl.when(sp > 0)
    def _():
        for copy in to_down:
            copy.wait_send()

    for small in smalls[1:]:
        small.wait()
    u_all = 0.77 * speed[...] * jnp.cos(heading[...])
    v_all = 0.77 * speed[...] * jnp.sin(heading[...])
    for r in range(rows):
        u_s[r] = u_all[r : r + 1]
        v_s[r] = v_all[r : r + 1]

    q_load.wait()
    turned = jnp.dot(
        reversal(nb, 0, nb, 0), q2[pl.ds(0, nb)], preferred_element_type=jnp.float32
    ).astype(jnp.bfloat16)
    for c in range(BINS // 256):
        q2[pl.ds(nb, nb), pl.ds(c * 256, 256)] = jnp.dot(
            turned, reversal(BINS, 0, 256, c * 256), preferred_element_type=jnp.float32
        ).astype(jnp.bfloat16)

    own = pl.ds(pl.multiple_of(b * nb, 16), nb)

    def compute(row):
        total = jnp.sum(every[row], axis=0, keepdims=True) * (1.0 / BINS)
        low = every[row].astype(jnp.bfloat16)
        coupled = jnp.dot(q2[...], low, preferred_element_type=jnp.float32)
        energy = every[row, own]
        along = tab[:, FCOS : FCOS + 1] * u_s[row] + tab[:, FSIN : FSIN + 1] * v_s[row]
        growth = GROWTH * jnp.maximum(along - 1.0, 0.0)
        rate = (
            growth
            + NONLINEAR * (coupled[:nb] + coupled[nb:])
            - DAMPING * tab[:, STEEP2 : STEEP2 + 1] * (total * total)
        )
        ext[HALO + row] = energy + TIME_STEP * (rate * energy)

    def unit_step(j, carry):
        @pl.when(j == 0)
        def _():
            for k in range(1, chips):
                for q in range(parts):
                    far_part(q, k, far_from(k)).wait_recv()

        @pl.when(alone(j))
        def _():
            for k in range(1, chips):
                far_copy(j, k, far_from(k)).wait_recv()

        @pl.when(paired(j))
        def _():
            for k in range(1, chips):
                far_pair(j, k, far_from(k)).wait_recv()

        for k in range(1, chips):
            near_copy(j, k, far_from(k)).start()
        near_copy(j, 0, sibling).wait_recv()
        for k in range(1, chips):
            near_copy(j, k, other(far_from(k))).wait_recv()
        for r in range(UNIT):
            compute(start_row(j) + r)

        @pl.when(lax.rem((j + 1) * UNIT, CHUNK) == 0)
        def _():
            to_bins(start_row(j) // CHUNK)

        return carry

    lax.fori_loop(0, last, unit_step, 0)

    for r in range(UNIT):
        for k in range(1, chips):
            far_last(r, k, far_from(k)).wait_recv()
            near_last(r, k, far_from(k)).start()
        near_last(r, 0, sibling).wait_recv()
        for k in range(1, chips):
            near_last(r, k, other(far_from(k))).wait_recv()
        compute(last_row + r)
    to_bins(last_row // CHUNK)

    def drain(j, carry):
        @pl.when(alone(j))
        def _():
            for k in range(1, chips):
                far_copy(j, k, b).wait_send()

        @pl.when(paired(j))
        def _():
            for k in range(1, chips):
                far_pair(j, k, b).wait_send()

        for k in range(1, chips):
            near_copy(j, k, far_from(k)).wait_send()
        near_copy(j, 0, b).wait_send()
        return carry

    lax.fori_loop(0, last, drain, 0)
    for r in range(UNIT):
        for k in range(1, chips):
            far_last(r, k, b).wait_send()
            near_last(r, k, far_from(k)).wait_send()
        near_last(r, 0, b).wait_send()
    for q in range(parts):
        for k in range(1, chips):
            far_part(q, k, b).wait_send()


def on_device(n, s, spectrum, sea_mask, wind_speed, wind_heading, quad):
    nb, rows, cols = spectrum.shape
    units, chips, chunks = rows // UNIT, n // 2, rows // CHUNK
    vmem = pl.BlockSpec(memory_space=pltpu.VMEM)
    hbm = pl.BlockSpec(memory_space=pl.ANY)
    return pl.pallas_call(
        functools.partial(kernel, n, s),
        out_shape=pltpu.VMEM((nb, rows, cols), jnp.float32),
        in_specs=[hbm] * 6,
        out_specs=vmem,
        scratch_shapes=[
            pltpu.VMEM((rows, cols), jnp.int32),
            pltpu.VMEM((rows, cols), jnp.float32),
            pltpu.VMEM((rows, cols), jnp.float32),
            pltpu.VMEM((rows + 2 * HALO, nb, cols), jnp.float32),
            pltpu.VMEM((rows + 2 * HALO, 1, cols), jnp.float32),
            pltpu.VMEM((rows, 1, cols), jnp.float32),
            pltpu.VMEM((rows, 1, cols), jnp.float32),
            pltpu.VMEM((rows, BINS, cols), jnp.float32),
            pltpu.VMEM((2 * nb, BINS), jnp.bfloat16),
            pltpu.VMEM((nb, 128), jnp.float32),
            pltpu.SemaphoreType.DMA((chunks + 2,)),
            pltpu.SemaphoreType.DMA((part_count(nb),)),
            pltpu.SemaphoreType.DMA((3,)),
            pltpu.SemaphoreType.DMA((4,)),
            pltpu.SemaphoreType.DMA((4,)),
            pltpu.SemaphoreType.DMA((units - 1 + UNIT, chips)),
            pltpu.SemaphoreType.DMA((units - 1 + UNIT, chips)),
            pltpu.SemaphoreType.DMA((units - 1 + UNIT, chips)),
            pltpu.SemaphoreType.DMA((units - 1 + UNIT, chips)),
            pltpu.SemaphoreType.DMA((part_count(nb), chips)),
            pltpu.SemaphoreType.DMA((part_count(nb), chips)),
        ],
        compiler_params=pltpu.CompilerParams(
            collective_id=0, has_side_effects=True, vmem_limit_bytes=56 * 1024 * 1024
        ),
        cost_estimate=pl.CostEstimate(
            flops=4 * nb * BINS * rows * cols, bytes_accessed=8 * nb * rows * cols, transcendentals=0
        ),
        name="wave_step",
    )(
        spectrum, sea_mask, wind_speed, wind_heading, quad, jnp.asarray(bin_tables()),
    )


def solution(mesh):
    return jax.shard_map(
        functools.partial(on_device, mesh.shape["bin"], mesh.shape["space"]),
        mesh=mesh,
        in_specs=(
            P("bin", "space", None),
            P("space", None),
            P("space", None),
            P("space", None),
            P(),
        ),
        out_specs=P("bin", "space", None),
        check_vma=False,
    )
```

```python
import functools
import math

import jax
import jax.numpy as jnp
import numpy as np
from jax import lax
from jax.experimental import pallas as pl
from jax.experimental.pallas import tpu as pltpu
from jax.sharding import PartitionSpec as P

FREQS = 32
DIRS = 24
BINS = 768

LOG_RATIO = math.log(1.1)
TWO_PI = 2.0 * math.pi
TIME_STEP = 0.2
NONLINEAR = 1.5
DAMPING = 2.0
GROWTH = 0.15

HALO = 3
CHUNK = 8
TILE = 2
UNIT = 2

AX, AY, XPOS, YPOS, FCOS, FSIN, STEEP2 = range(7)


def bin_tables():
    bins = np.arange(BINS)
    level = (bins // DIRS).astype(np.float64)
    direction = (bins % DIRS).astype(np.float64)
    frequency = 0.04 * np.exp(level * LOG_RATIO)
    courant = 0.65 * np.exp(-level * LOG_RATIO)
    theta = (direction + 0.5) * (TWO_PI / DIRS)
    cos_theta, sin_theta = np.cos(theta), np.sin(theta)
    top_freq = 0.04 * math.exp((FREQS - 1) * LOG_RATIO)
    table = np.zeros((BINS, 128), np.float32)
    table[:, AX] = np.abs(courant * cos_theta)
    table[:, AY] = np.abs(courant * sin_theta)
    table[:, XPOS] = cos_theta > 0
    table[:, YPOS] = sin_theta > 0
    table[:, FCOS] = frequency * cos_theta
    table[:, FSIN] = frequency * sin_theta
    table[:, STEEP2] = (frequency / top_freq) ** 2
    return table


def reversal(rows, row_start, cols, col_start):
    i = lax.broadcasted_iota(jnp.int32, (rows, cols), 0).astype(jnp.float32) + row_start
    j = lax.broadcasted_iota(jnp.int32, (rows, cols), 1).astype(jnp.float32) + col_start
    level = jnp.floor((i + 0.5) * (1.0 / DIRS))
    return jnp.where(i + j == 2 * DIRS * level + (DIRS - 1), 1.0, 0.0).astype(jnp.bfloat16)


def part_count(nb):
    return 4 if nb % 32 == 0 else 2


def kernel(
    n, s, spec, mask_h, speed_h, heading_h, quad, table, nat,
    mask, speed, heading, ext, mask_s, u_s, v_s, every, q2, tab,
    load_sem, first_sem, small_sem, halo_send, halo_recv, x_send, x_recv, f_send, f_recv, part_send, part_recv,
):
    nb, rows, cols = spec.shape
    tiles = rows // TILE
    chunks = rows // CHUNK
    parts = part_count(nb)
    width = nb // parts
    units = rows // UNIT
    chips = n // 2
    b = lax.axis_index("bin")
    sp = lax.axis_index("space")
    chip, core = b // 2, lax.rem(b, 2)
    sibling = chip * 2 + 1 - core

    def far_to(k):
        return lax.rem(chip + k, chips) * 2 + core

    def far_from(k):
        return lax.rem(chip + chips - k, chips) * 2 + core

    loads = [
        pltpu.make_async_copy(
            spec.at[:, pl.ds(c * CHUNK, CHUNK)], nat.at[:, pl.ds(c * CHUNK, CHUNK)],
            load_sem.at[c],
        )
        for c in range(2, chunks)
    ]
    firsts = [
        pltpu.make_async_copy(
            spec.at[pl.ds(q * width, width), pl.ds(0, 2 * CHUNK)],
            nat.at[pl.ds(q * width, width), pl.ds(0, 2 * CHUNK)],
            first_sem.at[q],
        )
        for q in range(parts)
    ]
    smalls = [
        pltpu.make_async_copy(source, target, small_sem.at[at])
        for at, (source, target) in enumerate(
            ((mask_h, mask), (speed_h, speed), (heading_h, heading))
        )
    ]
    firsts[0].start()
    smalls[0].start()
    for small in smalls[1:]:
        small.start()
    tab_load = pltpu.make_async_copy(
        table.at[pl.ds(pl.multiple_of(b * nb, 16), nb)], tab, load_sem.at[chunks]
    )
    tab_load.start()
    for load in firsts[1:] + loads:
        load.start()
    q_load = pltpu.make_async_copy(
        quad.at[pl.ds(pl.multiple_of(b * nb, 16), nb)], q2.at[pl.ds(0, nb)], load_sem.at[chunks + 1]
    )
    q_load.start()

    barrier = pltpu.get_barrier_semaphore()
    pl.semaphore_signal(barrier, 1, device_id={"bin": sibling})
    for k in range(1, chips):
        pl.semaphore_signal(barrier, 1, device_id={"bin": far_to(k)})

    @pl.when(sp > 0)
    def _():
        pl.semaphore_signal(barrier, 1, device_id={"space": sp - 1})

    @pl.when(sp < s - 1)
    def _():
        pl.semaphore_signal(barrier, 1, device_id={"space": sp + 1})

    smalls[0].wait()
    mask_f = mask[...].astype(jnp.float32)
    for r in range(rows):
        mask_s[HALO + r] = mask_f[r : r + 1]

    def to_rows(c, first=0, last=nb // 8):
        def group(g, carry):
            at = pl.ds(pl.multiple_of(g * 8, 8), 8)
            ext[pl.ds(HALO + c * CHUNK, CHUNK), at] = jnp.swapaxes(
                nat[at, pl.ds(c * CHUNK, CHUNK)], 0, 1
            )
            return carry

        lax.fori_loop(first, last, group, 0)

    def to_bins(c):
        def group(g, carry):
            at = pl.ds(pl.multiple_of(g * 8, 8), 8)
            nat[at, pl.ds(pl.multiple_of(c * CHUNK, CHUNK), CHUNK)] = jnp.swapaxes(
                ext[pl.ds(HALO + c * CHUNK, CHUNK), at], 0, 1
            )
            return carry

        lax.fori_loop(0, nb // 8, group, 0)

    up = {"space": sp + 1}
    down = {"space": sp - 1}
    to_up = [
        pltpu.make_async_remote_copy(
            ext.at[pl.ds(rows, HALO)], ext.at[pl.ds(0, HALO)],
            halo_send.at[0], halo_recv.at[0], device_id=up,
        ),
        pltpu.make_async_remote_copy(
            mask_s.at[pl.ds(rows, HALO)], mask_s.at[pl.ds(0, HALO)],
            halo_send.at[1], halo_recv.at[1], device_id=up,
        ),
    ]
    to_down = [
        pltpu.make_async_remote_copy(
            ext.at[pl.ds(HALO, HALO)], ext.at[pl.ds(rows + HALO, HALO)],
            halo_send.at[2], halo_recv.at[2], device_id=down,
        ),
        pltpu.make_async_remote_copy(
            mask_s.at[pl.ds(HALO, HALO)], mask_s.at[pl.ds(rows + HALO, HALO)],
            halo_send.at[3], halo_recv.at[3], device_id=down,
        ),
    ]

    def start_row(j):
        return lax.rem(j * UNIT + CHUNK, rows)

    last = units - 1
    ahead = units // 2
    last_row = (last * UNIT + CHUNK) % rows

    def block(row, count, owner):
        return every.at[pl.ds(row, count), pl.ds(pl.multiple_of(owner * nb, 16), nb)]

    def far_piece(row, count, j, k, owner):
        part = block(row, count, owner)
        return pltpu.make_async_remote_copy(
            part, part, x_send.at[j, k], x_recv.at[j, k], device_id={"bin": far_to(k)}
        )

    def near_piece(row, count, j, k, owner):
        part = block(row, count, owner)
        return pltpu.make_async_remote_copy(
            part, part, f_send.at[j, k], f_recv.at[j, k], device_id={"bin": sibling}
        )

    def far_copy(j, k, owner):
        return far_piece(start_row(j), UNIT, j, k, owner)

    def near_copy(j, k, owner):
        return near_piece(start_row(j), UNIT, j, k, owner)

    def far_last(r, k, owner):
        return far_piece(last_row + r, 1, last + r, k, owner)

    def near_last(r, k, owner):
        return near_piece(last_row + r, 1, last + r, k, owner)

    def far_part(q, k, owner):
        part = every.at[
            pl.ds(CHUNK, UNIT), pl.ds(pl.multiple_of(owner * nb + q * width, 8), width)
        ]
        return pltpu.make_async_remote_copy(
            part, part, part_send.at[q, k], part_recv.at[q, k], device_id={"bin": far_to(k)}
        )

    def other(owner):
        return owner + 1 - 2 * core

    tab_load.wait()
    lane = lax.broadcasted_iota(jnp.int32, (8, cols), 1)

    def propagate(t, first=0, last=nb // 8):
        base = t * TILE

        def group(g, carry):
            at = pl.multiple_of(g * 8, 8)
            coef = tab[pl.ds(at, 8)]

            def wide(col):
                return jnp.broadcast_to(coef[:, col : col + 1], (8, cols))

            ax, ay = wide(AX), wide(AY)
            xpos, ypos = wide(XPOS) > 0.5, wide(YPOS) > 0.5
            edge = jnp.where(
                jnp.where(ypos, lane, cols - 1 - lane) == 0, 0.0, 1.0
            )
            field = [ext[base + m, pl.ds(at, 8)] for m in range(TILE + 2 * HALO)]
            for step in range(3):
                new = []
                for m in range(1, len(field) - 1):
                    e = field[m]
                    back = jnp.where(xpos, field[m - 1], field[m + 1])
                    side = edge * jnp.where(
                        ypos, pltpu.roll(e, 1, 1), pltpu.roll(e, cols - 1, 1)
                    )
                    value = e - ax * (e - back) - ay * (e - side)
                    new.append(value * mask_s[base + m + step])
                field = new
            where = pl.multiple_of(b * nb + at, 8)
            for m in range(TILE):
                every[base + m, pl.ds(where, 8)] = field[m]
            return carry

        lax.fori_loop(first, last, group, 0)

    for q in range(parts):
        span = (q * width // 8, (q + 1) * width // 8)
        firsts[q].wait()
        for c in range(2):
            to_rows(c, *span)
        propagate(CHUNK // TILE, *span)
        if q == 0:
            pl.semaphore_wait(barrier, chips + jnp.minimum(sp, 1) + jnp.minimum(s - 1 - sp, 1))
        for k in range(1, chips):
            far_part(q, k, b).start()
    near_copy(0, 0, b).start()

    @pl.when(sp > 0)
    def _():
        for copy in to_down:
            copy.start()

    @pl.when(sp == 0)
    def _():
        ext[pl.ds(0, HALO)] = jnp.zeros((HALO, nb, cols), jnp.float32)
        mask_s[pl.ds(0, HALO)] = jnp.zeros((HALO, 1, cols), jnp.float32)

    @pl.when(sp == s - 1)
    def _():
        ext[pl.ds(rows + HALO, HALO)] = jnp.zeros((HALO, nb, cols), jnp.float32)
        mask_s[pl.ds(rows + HALO, HALO)] = jnp.zeros((HALO, 1, cols), jnp.float32)

    def tile_step(i, carry):
        t = lax.rem(i + CHUNK // TILE, tiles)

        for c in range(2, chunks):

            @pl.when(i == (c * CHUNK - HALO - CHUNK) // TILE)
            def _():
                loads[c - 2].wait()
                to_rows(c)

        @pl.when(i == (rows - CHUNK - HALO - CHUNK) // TILE)
        def _():
            @pl.when(sp < s - 1)
            def _():
                for copy in to_up:
                    copy.start()

        @pl.when(i == (rows - HALO - CHUNK) // TILE)
        def _():
            @pl.when(sp > 0)
            def _():
                for copy in to_up:
                    copy.wait_recv()

            @pl.when(sp < s - 1)
            def _():
                for copy in to_down:
                    copy.wait_recv()

        propagate(t)

        @pl.when(i < ahead)
        def _():
            for k in range(1, chips):
                far_copy(i, k, b).start()

        @pl.when(i < last)
        def _():
            near_copy(i, 0, b).start()

        @pl.when(i == last)
        def _():
            for r in range(UNIT):
                near_last(r, 0, b).start()

        return carry

    lax.fori_loop(1, tiles, tile_step, 0)

    @pl.when(sp < s - 1)
    def _():
        for copy in to_up:
            copy.wait_send()

    @pl.when(sp > 0)
    def _():
        for copy in to_down:
            copy.wait_send()

    for small in smalls[1:]:
        small.wait()
    u_all = 0.77 * speed[...] * jnp.cos(heading[...])
    v_all = 0.77 * speed[...] * jnp.sin(heading[...])
    for r in range(rows):
        u_s[r] = u_all[r : r + 1]
        v_s[r] = v_all[r : r + 1]

    q_load.wait()
    turned = jnp.dot(
        reversal(nb, 0, nb, 0), q2[pl.ds(0, nb)], preferred_element_type=jnp.float32
    ).astype(jnp.bfloat16)
    for c in range(BINS // 256):
        q2[pl.ds(nb, nb), pl.ds(c * 256, 256)] = jnp.dot(
            turned, reversal(BINS, 0, 256, c * 256), preferred_element_type=jnp.float32
        ).astype(jnp.bfloat16)

    own = pl.ds(pl.multiple_of(b * nb, 16), nb)

    def compute(row):
        total = jnp.sum(every[row], axis=0, keepdims=True) * (1.0 / BINS)
        low = every[row].astype(jnp.bfloat16)
        coupled = jnp.dot(q2[...], low, preferred_element_type=jnp.float32)
        energy = every[row, own]
        along = tab[:, FCOS : FCOS + 1] * u_s[row] + tab[:, FSIN : FSIN + 1] * v_s[row]
        growth = GROWTH * jnp.maximum(along - 1.0, 0.0)
        rate = (
            growth
            + NONLINEAR * (coupled[:nb] + coupled[nb:])
            - DAMPING * tab[:, STEEP2 : STEEP2 + 1] * (total * total)
        )
        ext[HALO + row] = energy + TIME_STEP * (rate * energy)

    def unit_step(j, carry):
        @pl.when(j == 0)
        def _():
            for k in range(1, chips):
                for q in range(parts):
                    far_part(q, k, far_from(k)).wait_recv()
                near_copy(j, k, far_from(k)).start()

        @pl.when(j > 0)
        def _():
            for k in range(1, chips):
                far_copy(j, k, far_from(k)).wait_recv()
                near_copy(j, k, far_from(k)).start()

        @pl.when(j + ahead < last)
        def _():
            for k in range(1, chips):
                far_copy(j + ahead, k, b).start()

        @pl.when(j + ahead == last)
        def _():
            for r in range(UNIT):
                for k in range(1, chips):
                    far_last(r, k, b).start()

        near_copy(j, 0, sibling).wait_recv()
        for k in range(1, chips):
            near_copy(j, k, other(far_from(k))).wait_recv()
        for r in range(UNIT):
            compute(start_row(j) + r)

        @pl.when(lax.rem((j + 1) * UNIT, CHUNK) == 0)
        def _():
            to_bins(start_row(j) // CHUNK)

        return carry

    lax.fori_loop(0, last, unit_step, 0)

    for r in range(UNIT):
        for k in range(1, chips):
            far_last(r, k, far_from(k)).wait_recv()
            near_last(r, k, far_from(k)).start()
        near_last(r, 0, sibling).wait_recv()
        for k in range(1, chips):
            near_last(r, k, other(far_from(k))).wait_recv()
        compute(last_row + r)
    to_bins(last_row // CHUNK)

    def drain(j, carry):
        @pl.when(j > 0)
        def _():
            for k in range(1, chips):
                far_copy(j, k, b).wait_send()

        for k in range(1, chips):
            near_copy(j, k, far_from(k)).wait_send()
        near_copy(j, 0, b).wait_send()
        return carry

    lax.fori_loop(0, last, drain, 0)
    for r in range(UNIT):
        for k in range(1, chips):
            far_last(r, k, b).wait_send()
            near_last(r, k, far_from(k)).wait_send()
        near_last(r, 0, b).wait_send()
    for q in range(parts):
        for k in range(1, chips):
            far_part(q, k, b).wait_send()


def on_device(n, s, spectrum, sea_mask, wind_speed, wind_heading, quad):
    nb, rows, cols = spectrum.shape
    units, chips, chunks = rows // UNIT, n // 2, rows // CHUNK
    vmem = pl.BlockSpec(memory_space=pltpu.VMEM)
    hbm = pl.BlockSpec(memory_space=pl.ANY)
    return pl.pallas_call(
        functools.partial(kernel, n, s),
        out_shape=pltpu.VMEM((nb, rows, cols), jnp.float32),
        in_specs=[hbm] * 6,
        out_specs=vmem,
        scratch_shapes=[
            pltpu.VMEM((rows, cols), jnp.int32),
            pltpu.VMEM((rows, cols), jnp.float32),
            pltpu.VMEM((rows, cols), jnp.float32),
            pltpu.VMEM((rows + 2 * HALO, nb, cols), jnp.float32),
            pltpu.VMEM((rows + 2 * HALO, 1, cols), jnp.float32),
            pltpu.VMEM((rows, 1, cols), jnp.float32),
            pltpu.VMEM((rows, 1, cols), jnp.float32),
            pltpu.VMEM((rows, BINS, cols), jnp.float32),
            pltpu.VMEM((2 * nb, BINS), jnp.bfloat16),
            pltpu.VMEM((nb, 128), jnp.float32),
            pltpu.SemaphoreType.DMA((chunks + 2,)),
            pltpu.SemaphoreType.DMA((part_count(nb),)),
            pltpu.SemaphoreType.DMA((3,)),
            pltpu.SemaphoreType.DMA((4,)),
            pltpu.SemaphoreType.DMA((4,)),
            pltpu.SemaphoreType.DMA((units - 1 + UNIT, chips)),
            pltpu.SemaphoreType.DMA((units - 1 + UNIT, chips)),
            pltpu.SemaphoreType.DMA((units - 1 + UNIT, chips)),
            pltpu.SemaphoreType.DMA((units - 1 + UNIT, chips)),
            pltpu.SemaphoreType.DMA((part_count(nb), chips)),
            pltpu.SemaphoreType.DMA((part_count(nb), chips)),
        ],
        compiler_params=pltpu.CompilerParams(
            collective_id=0, has_side_effects=True, vmem_limit_bytes=56 * 1024 * 1024
        ),
        cost_estimate=pl.CostEstimate(
            flops=4 * nb * BINS * rows * cols, bytes_accessed=8 * nb * rows * cols, transcendentals=0
        ),
        name="wave_step",
    )(
        spectrum, sea_mask, wind_speed, wind_heading, quad, jnp.asarray(bin_tables()),
    )


def solution(mesh):
    return jax.shard_map(
        functools.partial(on_device, mesh.shape["bin"], mesh.shape["space"]),
        mesh=mesh,
        in_specs=(
            P("bin", "space", None),
            P("space", None),
            P("space", None),
            P("space", None),
            P(),
        ),
        out_specs=P("bin", "space", None),
        check_vma=False,
    )
```
